32 devices in a mesh: stream: 8 (over z, y), cross: 4 (over x, core).
Axes of the slice: x: 2, y: 2, z: 4, core: 2. Of those that a mesh axis runs over, the one named last changes fastest.
Arguments:
- forcing: bfloat16 [24, 8, 144, 384], P('stream', 'cross'), may hold values from -1.1953125 to 1.1953125
- deformation_velocity: bfloat16 [24, 8, 144, 384], P('stream', 'cross'), may hold values from -6 to 6
- face_mask: int32 [4, 24, 8, 144], P(None, 'stream', 'cross'), may hold values 0 or 1
- lifting: bfloat16 [4, 384, 384], replicated, may hold values from -0.0625 to 0.0625
- inverse: bfloat16 [24, 8, 384, 384], P('stream', 'cross'), may hold values from -1 to 1
- retention: float32 [24, 384], P('stream'), may hold values from 0 to 1
Outputs:
- stress: float32 [24, 8, 144, 384], P('stream', 'cross')
The draws below stay inside these ranges and needn't reach their ends.
All inputs are finite; a program needn't handle non-finite values. No bound on the sum of `face_mask` on one device may be relied on, other than what follows from the above.
Results may differ from the reference program's by a relative error of at most 0.0039.
Values may be sent and summed in bfloat16 or wider, within the bound.
No kernel may reach another device: no remote copies, remote signals or barrier semaphores. Data moves between devices by JAX's collectives and lax.ppermute only.
A program may use at most 128 MiB of HBM per device.

```python
import math
import jax
import jax.numpy as jnp
from jax import lax

DOFS = 384
CB = 144
SLAB_TOTAL = 24
NA = 8


def draw_inverse(key, part):
    key = jax.random.fold_in(key, 7)
    key_diag, key_rest = jax.random.split(key)
    diagonal = jax.random.uniform(key_diag, (SLAB_TOTAL, NA, DOFS, 1), jnp.float32, 0.3, 0.7)
    off_diag = jnp.clip(jax.random.normal(key_rest, (SLAB_TOTAL, NA, DOFS, DOFS), jnp.float32), -4.0, 4.0)
    places = jnp.arange(DOFS)
    identity_mask = (places[:, None] == places[None, :]).astype(jnp.float32)
    matrix = identity_mask[None, None] * diagonal + (1.0 - identity_mask[None, None]) * off_diag * (0.3 / math.sqrt(DOFS))
    return matrix.astype(jnp.bfloat16)


def draw_retention(key, part):
    key = jax.random.fold_in(key, 11)
    seed_category, seed_dispersion, seed_surge, seed_dissipation = jax.random.split(key, 4)
    slow_count = 8
    slow = jax.random.randint(seed_category, (DOFS,), 0, 16) < slow_count
    spread = jax.random.uniform(seed_dispersion, (SLAB_TOTAL, DOFS), jnp.float32, 0.5, 1.0)
    slow_rate = spread * (math.log(10.0) / (3.0 * SLAB_TOTAL))
    fast_rate = spread / 20.0
    rates = jnp.where(slow[None, :], slow_rate, fast_rate)
    surging_slab_indices = jax.random.randint(seed_surge, (2,), 0, SLAB_TOTAL)
    layer_numbers = jnp.arange(SLAB_TOTAL)
    is_bursting = jnp.any(layer_numbers[:, None] == surging_slab_indices[None, :], axis=1)
    losses = jax.random.uniform(seed_dissipation, (SLAB_TOTAL, 1), jnp.float32, 0.2, 0.5)
    return jnp.exp(-rates) * jnp.where(is_bursting[:, None], 1.0 - losses, 1.0)


def touch_ends(drawn, own_key, smallest, top_value):
    longest = drawn.shape.index(max(drawn.shape))
    spots = []
    for shift in (0, 1):
        where = [jax.random.randint(jax.random.fold_in(own_key, axis), (), 0, length) for axis, length in enumerate(drawn.shape)]
        where[longest] = (where[longest] + shift) % drawn.shape[longest]
        spots.append(tuple(where))
    return drawn.at[spots[0]].set(smallest).at[spots[1]].set(top_value)


def block_levels(key, shape, pieces, low, high):
    loudness, own = 1.0, jax.random.fold_in(key, 6)
    for axis_at, blocks in pieces:
        steps = jnp.exp(jax.random.uniform(jax.random.fold_in(own, axis_at), (blocks,), jnp.float32, low / len(pieces), high / len(pieces)))
        loudness = loudness * jnp.repeat(steps, shape[axis_at] // blocks).reshape([-1 if axis == axis_at else 1 for axis in range(len(shape))])
    return loudness


def gaussian(own_key, shape, scale, bound, cuts=(), kind=jnp.bfloat16):
    loudness = block_levels(own_key, shape, cuts, -0.22, 0.18) if cuts else 1.0
    entries = jax.random.normal(own_key, shape, jnp.float32) * scale * loudness
    return jnp.minimum(jnp.maximum(entries, -bound), bound).astype(kind)


def setup_inputs(seed: int = 0) -> dict:
    streams_of = jax.random.split(jax.random.key(seed), 7)
    forcing = gaussian(streams_of[0], (SLAB_TOTAL, NA, CB, DOFS), 0.2, 1.1953125, ((0, 8), (1, 4)))
    deformation_velocity = gaussian(streams_of[1], (SLAB_TOTAL, NA, CB, DOFS), 1.0, 6.0, ((0, 8), (1, 4)))
    face_mask = touch_ends((jax.random.randint(streams_of[2], (4, SLAB_TOTAL, NA, CB), 0, 2) < 1).astype(jnp.int32), jax.random.fold_in(streams_of[2], 1), 0, 1)
    lifting = gaussian(streams_of[3], (4, DOFS, DOFS), (24 * DOFS) ** -0.5, 0.0625)
    inverse = draw_inverse(jax.random.fold_in(streams_of[6], 71), 0)
    retention = draw_retention(jax.random.fold_in(streams_of[6], 71), 0)
    return {"forcing": forcing, "deformation_velocity": deformation_velocity, "face_mask": face_mask, "lifting": lifting, "inverse": inverse, "retention": retention}


def reference(forcing, deformation_velocity, face_mask, lifting, inverse, retention):
    def layer_step(previous, inputs):
        forcing_layer, strain_layer, mask_layer, inverse_layer, keep_layer = inputs
        widened = strain_layer.astype(jnp.float32)
        padded = jnp.pad(widened, ((1, 1), (1, 1), (0, 0)))
        center = padded[1:-1, 1:-1]
        neighbours = (padded[:-2, 1:-1], padded[2:, 1:-1], padded[1:-1, :-2], padded[1:-1, 2:])
        source = forcing_layer.astype(jnp.float32).reshape(-1, DOFS)
        for face_index in range(4):
            jump_term = (mask_layer[face_index][:, :, None].astype(jnp.float32) * (neighbours[face_index] - center)).astype(jnp.bfloat16)
            source = source + jnp.dot(jump_term.reshape(-1, DOFS), lifting[face_index], preferred_element_type=jnp.float32)
        source_rows = source.astype(jnp.bfloat16).reshape(NA, CB, DOFS).astype(jnp.float32)
        solved = jnp.einsum("abd,ade->abe", source_rows, inverse_layer.astype(jnp.float32))
        current = keep_layer[None, None, :] * previous + solved
        return current, current

    masks_by_layer = jnp.moveaxis(face_mask, 1, 0)
    inflow = jnp.zeros((NA, CB, DOFS), jnp.float32)
    final, stresses = lax.scan(layer_step, inflow, (forcing, deformation_velocity, masks_by_layer, inverse, retention))
    return stresses
```

```python
import functools

import jax
import jax.numpy as jnp
from jax import lax
from jax.experimental import pallas as pl
from jax.experimental.pallas import tpu as pltpu
from jax.sharding import PartitionSpec as P

GROUP = 4
F32, BF16 = jnp.float32, jnp.bfloat16
VMEM_LIMIT = 48 * 1024 * 1024


def masked_jump(mask, neighbour, center):
    return (mask * (neighbour - center)).astype(BF16)


def along_b(cells):
    rows = lax.broadcasted_iota(jnp.int32, cells.shape, 0)
    last = cells.shape[0] - 1
    lower = jnp.where(rows == 0, 0.0, pltpu.roll(cells, 1, 0))
    upper = jnp.where(rows == last, 0.0, pltpu.roll(cells, last, 0))
    return lower, upper


def mask_columns(mask_ref, layer):
    rows = [mask_ref[face, layer, a : a + 1, :] for face in range(4) for a in range(2)]
    return jnp.concatenate(rows, axis=0).astype(F32).T


def dot(a, b):
    return jnp.dot(a, b, preferred_element_type=F32)


def inner_kernel(place, mask_ref, cells_ref, forcing_ref, halo_ref, lift_ref, inverse_ref, keep_ref, far_ref, near_ref, carry):
    layer = pl.program_id(0)
    odd = place[0]
    near_at, far_at = odd, 1 - odd
    columns = mask_columns(mask_ref, 0)
    is_odd = odd == 1

    def mask(face_even, a_even, face_odd, a_odd):
        even = columns[:, 2 * face_even + a_even : 2 * face_even + a_even + 1]
        other = columns[:, 2 * face_odd + a_odd : 2 * face_odd + a_odd + 1]
        return jnp.where(is_odd, other, even)

    far = cells_ref[0, far_at].astype(F32)
    near = cells_ref[0, near_at].astype(F32)
    halo = halo_ref[0].astype(F32)
    outer_face, inner_face = 1 - odd, odd
    far_low, far_up = along_b(far)
    near_low, near_up = along_b(near)
    far_source = forcing_ref[0, far_at].astype(F32)
    near_source = forcing_ref[0, near_at].astype(F32)
    pairs = (
        (masked_jump(mask(1, 1, 0, 0), halo, far), masked_jump(mask(1, 0, 0, 1), far, near), lift_ref[outer_face]),
        (masked_jump(mask(2, 1, 2, 0), far_low, far), masked_jump(mask(2, 0, 2, 1), near_low, near), lift_ref[2]),
        (masked_jump(mask(3, 1, 3, 0), far_up, far), masked_jump(mask(3, 0, 3, 1), near_up, near), lift_ref[3]),
    )
    far_source = far_source + dot(masked_jump(mask(0, 1, 1, 0), near, far), lift_ref[inner_face])
    for far_jump, near_jump, matrix in pairs:
        far_source = far_source + dot(far_jump, matrix)
        near_source = near_source + dot(near_jump, matrix)
    near_ref[0] = near_source
    solved = dot(far_source.astype(BF16), inverse_ref[0, 0])

    @pl.when(layer == 0)
    def _():
        carry[...] = solved

    @pl.when(layer > 0)
    def _():
        carry[...] = keep_ref[pl.ds(layer, 1), :] * carry[...] + solved

    far_ref[0] = carry[...]


def outer_kernel(place, mask_ref, cells_ref, halo_ref, source_ref, lift_ref, inverse_ref, keep_ref, far_ref, near_ref, p0, p1, p2, p3, carry):
    layer = pl.program_id(0)
    layers = pl.num_programs(0)
    odd = place[0]
    columns = mask_columns(mask_ref, 0)
    mask = jnp.where(odd == 1, columns[:, 3:4], columns[:, 0:1])
    near = cells_ref[0, 0].astype(F32)
    jump = masked_jump(mask, halo_ref[0].astype(F32), near)
    source = source_ref[0] + dot(jump, lift_ref[0])
    solved = dot(source.astype(BF16), inverse_ref[0, 0])
    rows = near.shape[0]
    mine = pl.ds(rows, rows)

    @pl.when(layer == 0)
    def _():
        carry[mine, :] = solved

    @pl.when(layer > 0)
    def _():
        carry[mine, :] = keep_ref[pl.ds(layer, 1), :] * carry[mine, :] + solved

    near_ref[0] = carry[mine, :]

    @pl.when(layer == layers - 1)
    def _():
        carry[pl.ds(0, rows), :] = far_ref[0]
        factor = keep_ref[0:1, :]
        for at in range(1, keep_ref.shape[0]):
            factor = factor * keep_ref[at : at + 1, :]
        high = factor.astype(BF16).astype(F32)
        low = factor - high
        at = lax.broadcasted_iota(jnp.int32, (8, factor.shape[1]), 0)
        extra = jnp.where(at == 0, high, jnp.where(at == 1, low, 0.0))
        piece = 2 * rows // GROUP
        for k, out in enumerate((p0, p1, p2, p3)):
            start = pl.multiple_of((place[1] ^ k) * piece, 8)
            out[...] = jnp.concatenate([carry[pl.ds(start, piece), :], extra], axis=0).astype(BF16)


def final_kernel(place, far_ref, near_ref, keep_ref, e0, e1, e2, e3, out_ref, incoming):
    layer = pl.program_id(0)
    rows = far_ref.shape[1]
    odd = place[0]
    piece = e0.shape[0]

    @pl.when(layer == 0)
    def _():
        for k, part in enumerate((e0, e1, e2, e3)):
            start = pl.multiple_of((place[1] ^ k) * piece, 8)
            incoming[pl.ds(start, piece), :] = part[...].astype(F32)

    incoming[...] = keep_ref[pl.ds(layer, 1), :] * incoming[...]
    out_ref[0, 1 - odd] = far_ref[0] + incoming[pl.ds(0, rows), :]
    out_ref[0, odd] = near_ref[0] + incoming[pl.ds(rows, rows), :]


def call(kernel, place, operands, in_specs, outs, out_specs, layers, scratch, flops, moved):
    return pl.pallas_call(
        kernel,
        out_shape=outs,
        grid_spec=pltpu.PrefetchScalarGridSpec(
            num_scalar_prefetch=1, grid=(layers,), in_specs=in_specs, out_specs=out_specs, scratch_shapes=scratch
        ),
        compiler_params=pltpu.CompilerParams(dimension_semantics=("arbitrary",), vmem_limit_bytes=VMEM_LIMIT),
        cost_estimate=pl.CostEstimate(flops=flops, bytes_accessed=moved, transcendentals=0),
    )(place, *operands)


def body(forcing, cells, face_mask, lifting, inverse, retention):
    layers, _, width, dofs = cells.shape
    crosses, streams = lax.axis_size("cross"), lax.axis_size("stream")
    cross, stream = lax.axis_index("cross"), lax.axis_index("stream")
    odd, member = cross % 2, stream % GROUP
    place = jnp.stack([odd, member]).astype(jnp.int32)

    outward = jnp.where(odd == 1, cells[:, 0], cells[:, 1])
    across = jnp.where(odd == 1, cells[:, 1], cells[:, 0])
    core_halo = lax.ppermute(outward, "cross", [(i, i ^ 1) for i in range(crosses)])
    links = [pair for i in range(1, crosses - 1, 2) for pair in ((i, i + 1), (i + 1, i))]
    chip_halo = lax.ppermute(across, "cross", links)

    row = lambda at: pl.BlockSpec((1, 1, width, dofs), lambda l, s, at=at: (l, at(s), 0, 0))
    both = pl.BlockSpec((1, 2, width, dofs), lambda l, s: (l, 0, 0, 0))
    single = pl.BlockSpec((1, width, dofs), lambda l, s: (l, 0, 0))
    masks = pl.BlockSpec((4, 1, 2, width), lambda l, s: (0, l, 0, 0))
    keeps = pl.BlockSpec((layers, dofs), lambda l, s: (0, 0))
    square = lambda at: pl.BlockSpec((1, 1, dofs, dofs), lambda l, s, at=at: (l, at(s), 0, 0))
    near_at = lambda s: s[0]
    far_at = lambda s: 1 - s[0]
    stack = jax.ShapeDtypeStruct((layers, width, dofs), F32)
    unit = 2 * layers * width * dofs * dofs

    far, near_source = call(
        inner_kernel,
        place,
        (face_mask, cells, forcing, core_halo, lifting, inverse, retention),
        [masks, both, both, single, pl.BlockSpec((4, dofs, dofs), lambda l, s: (0, 0, 0)), square(far_at), keeps],
        (stack, stack),
        (single, single),
        layers,
        [pltpu.VMEM((width, dofs), F32)],
        8 * unit,
        8_000_000,
    )

    piece = 2 * width // GROUP
    payload = jax.ShapeDtypeStruct((piece + 8, dofs), BF16)
    whole = pl.BlockSpec((piece + 8, dofs), lambda l, s: (0, 0))
    near, *pieces = call(
        outer_kernel,
        place,
        (face_mask, cells, chip_halo, near_source, lifting, inverse, retention, far),
        [
            masks,
            row(near_at),
            single,
            single,
            pl.BlockSpec((1, dofs, dofs), lambda l, s: (s[0], 0, 0)),
            square(near_at),
            keeps,
            pl.BlockSpec((1, width, dofs), lambda l, s: (layers - 1, 0, 0)),
        ],
        (stack,) + (payload,) * GROUP,
        (single,) + (whole,) * GROUP,
        layers,
        [pltpu.VMEM((2 * width, dofs), F32)],
        2 * unit,
        3_000_000,
    )

    def swap(part, distance):
        return lax.ppermute(part, "stream", [(i, i ^ distance) for i in range(streams)])

    got = [pieces[0]] + [swap(pieces[k], k) for k in range(1, GROUP)]
    pick = lambda parts, j: functools.reduce(
        lambda rest, k: jnp.where((member ^ k) == j, parts[k], rest), range(1, GROUP), parts[0]
    )
    ordered = [pick(got, j).astype(F32) for j in range(GROUP)]
    values = [part[:piece] for part in ordered]
    factors = [part[piece : piece + 1] + part[piece + 1 : piece + 2] for part in ordered]

    total, total_factor = values[0], factors[0]
    for j in range(1, GROUP):
        total = factors[j] * total + values[j]
        total_factor = total_factor * factors[j]
    before, before_factor = jnp.zeros_like(total), jnp.ones_like(total_factor)
    distance = GROUP
    while distance < streams:
        last = 2 * distance >= streams
        if last:
            met = swap(total.astype(BF16), distance).astype(F32)
        else:
            high = total_factor.astype(BF16)
            low = (total_factor - high.astype(F32)).astype(BF16)
            met = swap(jnp.concatenate([total.astype(BF16), high, low], axis=0), distance).astype(F32)
        later = (stream & distance) != 0
        before = jnp.where(later, before_factor * met[:piece] + before, before)
        if not last:
            met_factor = met[piece : piece + 1] + met[piece + 1 : piece + 2]
            before_factor = jnp.where(later, before_factor * met_factor, before_factor)
            total = jnp.where(later, total_factor * met[:piece] + total, met_factor * total + met[:piece])
            total_factor = total_factor * met_factor
        distance *= 2

    entering = [before]
    for j in range(GROUP - 1):
        entering.append(factors[j] * entering[j] + values[j])
    entering = [part.astype(BF16) for part in entering]
    give = [pick(entering, k) for k in range(GROUP)]
    back = [give[0]] + [swap(give[k], k) for k in range(1, GROUP)]

    part = pl.BlockSpec((piece, dofs), lambda l, s: (0, 0))
    return call(
        final_kernel,
        place,
        (far, near, retention, *back),
        [single, single, keeps] + [part] * GROUP,
        jax.ShapeDtypeStruct((layers, 2, width, dofs), F32),
        both,
        layers,
        [pltpu.VMEM((2 * width, dofs), F32)],
        1_000_000,
        4_000_000,
    )


def solution(mesh):
    return jax.shard_map(
        body,
        mesh=mesh,
        in_specs=(
            P("stream", "cross", None, None),
            P("stream", "cross", None, None),
            P(None, "stream", "cross", None),
            P(),
            P("stream", "cross", None, None),
            P("stream", None),
        ),
        out_specs=P("stream", "cross", None, None),
        check_vma=False,
    )
```

```python
import functools

import jax
import jax.numpy as jnp
from jax import lax
from jax.experimental import pallas as pl
from jax.experimental.pallas import tpu as pltpu
from jax.sharding import PartitionSpec as P

GROUP = 4
F32, BF16 = jnp.float32, jnp.bfloat16
VMEM_LIMIT = 24 * 1024 * 1024
MASK_COST = 10_000_000_000


def masked_jump(mask, neighbour, center):
    return (mask * (neighbour - center)).astype(BF16)


def along_b(cells):
    rows = lax.broadcasted_iota(jnp.int32, cells.shape, 0)
    last = cells.shape[0] - 1
    lower = jnp.where(rows == 0, 0.0, pltpu.roll(cells, 1, 0))
    upper = jnp.where(rows == last, 0.0, pltpu.roll(cells, last, 0))
    return lower, upper


def mask_columns(mask_ref, layer):
    rows = [mask_ref[face, layer, a : a + 1, :] for face in range(4) for a in range(2)]
    rows.append(jnp.zeros((120, rows[0].shape[1]), rows[0].dtype))
    return jnp.concatenate(rows, axis=0).astype(F32).T


def dot(a, b):
    return jnp.dot(a, b, preferred_element_type=F32)


def mask_kernel(place, mask_ref, after, columns_ref):
    for l in range(columns_ref.shape[0]):
        columns_ref[l] = mask_columns(mask_ref, l)


def inner_kernel(place, columns_ref, halo_ref, keep_ref, near_row, far_row, forcing, lift, inverse, far_ref, source_ref):
    layers, width, dofs = near_row.shape
    odd = place[0]
    near_at, far_at = odd, 1 - odd
    is_odd = odd == 1
    carry = None
    for l in range(layers):
        columns = columns_ref[l]
        column = lambda face, even, other: jnp.where(
            is_odd, columns[:, 2 * face[1] + other : 2 * face[1] + other + 1], columns[:, 2 * face[0] + even : 2 * face[0] + even + 1]
        )
        near, far = near_row[l].astype(F32), far_row[l].astype(F32)
        near_low, near_up = along_b(near)
        far_low, far_up = along_b(far)
        halo = halo_ref[l].astype(F32)
        far_source = forcing[l, far_at].astype(F32)
        near_source = forcing[l, near_at].astype(F32)
        pairs = (
            (masked_jump(column((1, 0), 1, 0), halo, far), masked_jump(column((1, 0), 0, 1), far, near), lift[1 - odd]),
            (masked_jump(column((2, 2), 1, 0), far_low, far), masked_jump(column((2, 2), 0, 1), near_low, near), lift[2]),
            (masked_jump(column((3, 3), 1, 0), far_up, far), masked_jump(column((3, 3), 0, 1), near_up, near), lift[3]),
        )
        lifted = sum(dot(jnp.concatenate(pair[:2], axis=0), pair[2]) for pair in pairs)
        inner = masked_jump(column((0, 1), 1, 0), near, far)
        far_source = far_source + lifted[:width] + dot(inner, lift[odd])
        source_ref[l] = near_source + lifted[width:]
        solved = dot(far_source.astype(BF16), inverse[l, far_at])
        carry = solved if l == 0 else keep_ref[l : l + 1, :] * carry + solved
        far_ref[l] = carry


def outer_kernel(place, halo_ref, columns_ref, near_row, source_ref, lift, inverse, keep_ref, far_ref, near_ref, p0, p1, p2, p3, carry):
    layers, width, dofs = near_row.shape
    odd = place[0]
    inside = place[2] == 0
    jumps = []
    for l in range(layers):
        edge = jnp.where(odd == 1, columns_ref[l, :, 3:4], columns_ref[l, :, 0:1])
        halo = jnp.where(inside, halo_ref[l].astype(F32), 0.0)
        jumps.append(masked_jump(edge, halo, near_row[l].astype(F32)))
    lifted = dot(jnp.concatenate(jumps, axis=0), lift[odd])
    total = None
    for l in range(layers):
        source = source_ref[l] + lifted[l * width : (l + 1) * width]
        solved = dot(source.astype(BF16), inverse[l, odd])
        total = solved if l == 0 else keep_ref[l : l + 1, :] * total + solved
        near_ref[l] = total
    carry[pl.ds(0, width), :] = far_ref[layers - 1]
    carry[pl.ds(width, width), :] = total
    factor = keep_ref[0:1, :]
    for l in range(1, layers):
        factor = factor * keep_ref[l : l + 1, :]
    high = factor.astype(BF16).astype(F32)
    low = factor - high
    at = lax.broadcasted_iota(jnp.int32, (8, dofs), 0)
    extra = jnp.where(at == 0, high, jnp.where(at == 1, low, 0.0))
    piece = 2 * width // GROUP
    for k, out in enumerate((p0, p1, p2, p3)):
        start = pl.multiple_of((place[1] ^ k) * piece, 8)
        out[...] = jnp.concatenate([carry[pl.ds(start, piece), :], extra], axis=0).astype(BF16)


def final_kernel(place, far_ref, near_ref, keep_ref, e0, e1, e2, e3, out_hbm, incoming, out, sem):
    layers, width, dofs = far_ref.shape
    odd = place[0]
    piece = e0.shape[0]
    for k, part in enumerate((e0, e1, e2, e3)):
        start = pl.multiple_of((place[1] ^ k) * piece, 8)
        incoming[pl.ds(start, piece), :] = part[...].astype(F32)
    copies = []
    factor = None
    for l in range(layers):
        factor = keep_ref[l : l + 1, :] if l == 0 else factor * keep_ref[l : l + 1, :]
        out[l, 1 - odd] = far_ref[l] + factor * incoming[pl.ds(0, width), :]
        out[l, odd] = near_ref[l] + factor * incoming[pl.ds(width, width), :]
        copies.append(pltpu.make_async_copy(out.at[l], out_hbm.at[l], sem.at[l]))
        copies[-1].start()
    for copy in copies:
        copy.wait()


def call(kernel, place, operands, in_specs, outs, out_specs, scratch, flops, moved):
    return pl.pallas_call(
        kernel,
        out_shape=outs,
        in_specs=[pl.BlockSpec(memory_space=pltpu.SMEM)] + in_specs,
        out_specs=out_specs,
        scratch_shapes=scratch,
        compiler_params=pltpu.CompilerParams(vmem_limit_bytes=VMEM_LIMIT),
        cost_estimate=pl.CostEstimate(flops=flops, bytes_accessed=moved, transcendentals=0),
    )(place, *operands)


def body(forcing, cells, face_mask, lifting, inverse, retention):
    layers, _, width, dofs = cells.shape
    crosses, streams = lax.axis_size("cross"), lax.axis_size("stream")
    cross, stream = lax.axis_index("cross"), lax.axis_index("stream")
    odd, member = cross % 2, stream % GROUP
    at_end = (cross == 0) | (cross == crosses - 1)
    place = jnp.stack([odd, member, at_end.astype(jnp.int32)]).astype(jnp.int32)

    links = []
    for s in range(streams):
        for c in range(crosses):
            other = (s ^ 1, c) if c in (0, crosses - 1) else (s, c + 1 if c % 2 else c - 1)
            links.append((s * crosses + c, other[0] * crosses + other[1]))
    vmem, hbm = pl.BlockSpec(memory_space=pltpu.VMEM), pl.BlockSpec(memory_space=pl.ANY)
    like = jax.ShapeDtypeStruct
    stack = like((layers, width, dofs), F32)
    slab = like((layers, width, dofs), BF16)
    unit = 2 * layers * width * dofs * dofs

    near_row = lax.dynamic_index_in_dim(cells, odd, 1, False)
    far_row = lax.dynamic_index_in_dim(cells, 1 - odd, 1, False)
    core_halo = lax.ppermute(far_row, "cross", [(i, i ^ 1) for i in range(crosses)])
    chip_halo = lax.ppermute(near_row, ("stream", "cross"), links)
    columns = call(
        mask_kernel, place, (face_mask, near_row), [vmem, hbm], like((layers, width, 128), F32), vmem, [], MASK_COST, 20_000_000
    )
    far, near_source = call(
        inner_kernel,
        place,
        (columns, core_halo, retention, near_row, far_row, forcing, lifting, inverse),
        [vmem] * 8,
        (stack, stack),
        (vmem,) * 2,
        [],
        9 * unit,
        5_000_000,
    )

    piece = 2 * width // GROUP
    near, *pieces = call(
        outer_kernel,
        place,
        (chip_halo, columns, near_row, near_source, lifting, inverse, retention, far),
        [vmem] * 8,
        (stack,) + (like((piece + 8, dofs), BF16),) * GROUP,
        (vmem,) * (1 + GROUP),
        [pltpu.VMEM((2 * width, dofs), F32)],
        2 * unit,
        3_000_000,
    )

    def swap(part, distance):
        return lax.ppermute(part, "stream", [(i, i ^ distance) for i in range(streams)])

    got = [pieces[0]] + [swap(pieces[k], k) for k in range(1, GROUP)]
    pick = lambda parts, j: functools.reduce(
        lambda rest, k: jnp.where((member ^ k) == j, parts[k], rest), range(1, GROUP), parts[0]
    )
    ordered = [pick(got, j).astype(F32) for j in range(GROUP)]
    values = [part[:piece] for part in ordered]
    factors = [part[piece : piece + 1] + part[piece + 1 : piece + 2] for part in ordered]

    total, total_factor = values[0], factors[0]
    for j in range(1, GROUP):
        total = factors[j] * total + values[j]
        total_factor = total_factor * factors[j]
    before, before_factor = jnp.zeros_like(total), jnp.ones_like(total_factor)
    distance = GROUP
    while distance < streams:
        last = 2 * distance >= streams
        if last:
            met = swap(total.astype(BF16), distance).astype(F32)
        else:
            high = total_factor.astype(BF16)
            low = (total_factor - high.astype(F32)).astype(BF16)
            met = swap(jnp.concatenate([total.astype(BF16), high, low], axis=0), distance).astype(F32)
        later = (stream & distance) != 0
        before = jnp.where(later, before_factor * met[:piece] + before, before)
        if not last:
            met_factor = met[piece : piece + 1] + met[piece + 1 : piece + 2]
            before_factor = jnp.where(later, before_factor * met_factor, before_factor)
            total = jnp.where(later, total_factor * met[:piece] + total, met_factor * total + met[:piece])
            total_factor = total_factor * met_factor
        distance *= 2

    entering = [before]
    for j in range(GROUP - 1):
        entering.append(factors[j] * entering[j] + values[j])
    entering = [part.astype(BF16) for part in entering]
    give = [pick(entering, k) for k in range(GROUP)]
    back = [give[0]] + [swap(give[k], k) for k in range(1, GROUP)]

    return call(
        final_kernel,
        place,
        (far, near, retention, *back),
        [vmem] * (3 + GROUP),
        like(cells.shape, F32),
        hbm,
        [pltpu.VMEM((2 * width, dofs), F32), pltpu.VMEM(cells.shape, F32), pltpu.SemaphoreType.DMA((layers,))],
        1_000_000,
        4_000_000,
    )


def solution(mesh):
    return jax.shard_map(
        body,
        mesh=mesh,
        in_specs=(
            P("stream", "cross", None, None),
            P("stream", "cross", None, None),
            P(None, "stream", "cross", None),
            P(),
            P("stream", "cross", None, None),
            P("stream", None),
        ),
        out_specs=P("stream", "cross", None, None),
        check_vma=False,
    )
```

```python
import functools

import jax
import jax.numpy as jnp
from jax import lax
from jax.experimental import pallas as pl
from jax.experimental.pallas import tpu as pltpu
from jax.sharding import PartitionSpec as P

GROUP = 4
F32, BF16 = jnp.float32, jnp.bfloat16
VMEM_LIMIT = 24 * 1024 * 1024
MASK_COST = 10_000_000_000


def masked_jump(mask, neighbour, center):
    return (mask * (neighbour - center)).astype(BF16)


def along_b(cells):
    rows = lax.broadcasted_iota(jnp.int32, cells.shape, 0)
    last = cells.shape[0] - 1
    lower = jnp.where(rows == 0, 0.0, pltpu.roll(cells, 1, 0))
    upper = jnp.where(rows == last, 0.0, pltpu.roll(cells, last, 0))
    return lower, upper


def mask_columns(mask_ref, layer):
    rows = [mask_ref[face, layer, a : a + 1, :] for face in range(4) for a in range(2)]
    rows.append(jnp.zeros((120, rows[0].shape[1]), rows[0].dtype))
    return jnp.concatenate(rows, axis=0).astype(F32).T


def dot(a, b):
    return jnp.dot(a, b, preferred_element_type=F32)


def mask_kernel(place, mask_ref, after, columns_ref):
    for l in range(columns_ref.shape[0]):
        columns_ref[l] = mask_columns(mask_ref, l)


def inner_kernel(place, columns_ref, halo_ref, keep_ref, near_row, far_row, forcing, lift, inverse, far_ref, source_ref, jumps):
    layers, width, dofs = near_row.shape
    odd = place[0]
    near_at, far_at = odd, 1 - odd
    is_odd = odd == 1
    outward = pl.ds(pl.multiple_of((1 - odd) * dofs, 128), dofs)
    inward = pl.ds(pl.multiple_of(odd * dofs, 128), dofs)
    weights = lift[...].reshape(4 * dofs, dofs)
    carry = None
    for l in range(layers):
        columns = columns_ref[l]
        column = lambda face, even, other: jnp.where(
            is_odd, columns[:, 2 * face[1] + other : 2 * face[1] + other + 1], columns[:, 2 * face[0] + even : 2 * face[0] + even + 1]
        )
        near, far = near_row[l].astype(F32), far_row[l].astype(F32)
        far_at_rows = pl.ds(2 * l * width, width)
        near_at_rows = pl.ds((2 * l + 1) * width, width)
        step = near - far
        jumps[far_at_rows, outward] = masked_jump(column((1, 0), 1, 0), halo_ref[l].astype(F32), far)
        jumps[far_at_rows, inward] = (column((0, 1), 1, 0) * step).astype(BF16)
        jumps[near_at_rows, outward] = (column((1, 0), 0, 1) * -step).astype(BF16)
        jumps[near_at_rows, inward] = jnp.zeros((width, dofs), BF16)
        for at, cells, even in ((far_at_rows, far, 1), (near_at_rows, near, 0)):
            low, up = along_b(cells)
            jumps[at, pl.ds(2 * dofs, dofs)] = masked_jump(column((2, 2), even, 1 - even), low, cells)
            jumps[at, pl.ds(3 * dofs, dofs)] = masked_jump(column((3, 3), even, 1 - even), up, cells)
        lifted = dot(jumps[pl.ds(2 * l * width, 2 * width), :], weights)
        source_ref[l] = forcing[l, near_at].astype(F32) + lifted[width:]
        far_source = forcing[l, far_at].astype(F32) + lifted[:width]
        solved = dot(far_source.astype(BF16), inverse[l, far_at])
        carry = solved if l == 0 else keep_ref[l : l + 1, :] * carry + solved
        far_ref[l] = carry


def outer_kernel(place, halo_ref, columns_ref, near_row, source_ref, lift, inverse, keep_ref, far_ref, near_ref, p0, p3, p2, p1, carry):
    layers, width, dofs = near_row.shape
    odd = place[0]
    inside = place[2] == 0
    jumps = []
    for l in range(layers):
        edge = jnp.where(odd == 1, columns_ref[l, :, 3:4], columns_ref[l, :, 0:1])
        halo = jnp.where(inside, halo_ref[l].astype(F32), 0.0)
        jumps.append(masked_jump(edge, halo, near_row[l].astype(F32)))
    lifted = dot(jnp.concatenate(jumps, axis=0), lift[odd])
    total = None
    for l in range(layers):
        source = source_ref[l] + lifted[l * width : (l + 1) * width]
        solved = dot(source.astype(BF16), inverse[l, odd])
        total = solved if l == 0 else keep_ref[l : l + 1, :] * total + solved
        near_ref[l] = total
    carry[pl.ds(0, width), :] = far_ref[layers - 1]
    carry[pl.ds(width, width), :] = total
    factor = keep_ref[0:1, :]
    for l in range(1, layers):
        factor = factor * keep_ref[l : l + 1, :]
    high = factor.astype(BF16).astype(F32)
    low = factor - high
    at = lax.broadcasted_iota(jnp.int32, (8, dofs), 0)
    extra = jnp.where(at == 0, high, jnp.where(at == 1, low, 0.0))
    piece = 2 * width // GROUP
    for k, out in enumerate((p0, p1, p2, p3)):
        start = pl.multiple_of((place[1] ^ k) * piece, 8)
        out[...] = jnp.concatenate([carry[pl.ds(start, piece), :], extra], axis=0).astype(BF16)


def final_kernel(place, far_ref, near_ref, keep_ref, e3, e2, e1, e0, out_hbm, incoming, out, sem):
    layers, width, dofs = far_ref.shape
    odd = place[0]
    piece = e0.shape[0]
    for k, part in enumerate((e0, e1, e2, e3)):
        start = pl.multiple_of((place[1] ^ k) * piece, 8)
        incoming[pl.ds(start, piece), :] = part[...].astype(F32)
    copies = []
    factor = None
    for l in range(layers):
        factor = keep_ref[l : l + 1, :] if l == 0 else factor * keep_ref[l : l + 1, :]
        out[l, 1 - odd] = far_ref[l] + factor * incoming[pl.ds(0, width), :]
        out[l, odd] = near_ref[l] + factor * incoming[pl.ds(width, width), :]
        copies.append(pltpu.make_async_copy(out.at[l], out_hbm.at[l], sem.at[l]))
        copies[-1].start()
    for copy in copies:
        copy.wait()


def call(kernel, place, operands, in_specs, outs, out_specs, scratch, flops, moved):
    return pl.pallas_call(
        kernel,
        out_shape=outs,
        in_specs=[pl.BlockSpec(memory_space=pltpu.SMEM)] + in_specs,
        out_specs=out_specs,
        scratch_shapes=scratch,
        compiler_params=pltpu.CompilerParams(vmem_limit_bytes=VMEM_LIMIT),
        cost_estimate=pl.CostEstimate(flops=flops, bytes_accessed=moved, transcendentals=0),
    )(place, *operands)


def body(forcing, cells, face_mask, lifting, inverse, retention):
    layers, _, width, dofs = cells.shape
    crosses, streams = lax.axis_size("cross"), lax.axis_size("stream")
    cross, stream = lax.axis_index("cross"), lax.axis_index("stream")
    odd, member = cross % 2, stream % GROUP
    at_end = (cross == 0) | (cross == crosses - 1)
    place = jnp.stack([odd, member, at_end.astype(jnp.int32)]).astype(jnp.int32)

    links = []
    for s in range(streams):
        for c in range(crosses):
            other = (s ^ 1, c) if c in (0, crosses - 1) else (s, c + 1 if c % 2 else c - 1)
            links.append((s * crosses + c, other[0] * crosses + other[1]))
    vmem, hbm = pl.BlockSpec(memory_space=pltpu.VMEM), pl.BlockSpec(memory_space=pl.ANY)
    like = jax.ShapeDtypeStruct
    stack = like((layers, width, dofs), F32)
    slab = like((layers, width, dofs), BF16)
    unit = 2 * layers * width * dofs * dofs

    near_row = lax.dynamic_index_in_dim(cells, odd, 1, False)
    far_row = lax.dynamic_index_in_dim(lax.optimization_barrier(cells), 1 - odd, 1, False)
    chip_halo = lax.ppermute(near_row, ("stream", "cross"), links)
    core_halo = lax.ppermute(far_row, "cross", [(i, i ^ 1) for i in range(crosses)])
    columns = call(
        mask_kernel, place, (face_mask, near_row), [vmem, hbm], like((layers, width, 128), F32), vmem, [], MASK_COST, 20_000_000
    )
    far, near_source = call(
        inner_kernel,
        place,
        (columns, core_halo, retention, near_row, far_row, forcing, lifting, inverse),
        [vmem] * 8,
        (stack, stack),
        (vmem,) * 2,
        [pltpu.VMEM((2 * layers * width, 4 * dofs), BF16)],
        9 * unit,
        5_000_000,
    )

    piece = 2 * width // GROUP
    near, piece0, piece3, piece2, piece1 = call(
        outer_kernel,
        place,
        (chip_halo, columns, near_row, near_source, lifting, inverse, retention, far),
        [vmem] * 8,
        (stack,) + (like((piece + 8, dofs), BF16),) * GROUP,
        (vmem,) * (1 + GROUP),
        [pltpu.VMEM((2 * width, dofs), F32)],
        2 * unit,
        3_000_000,
    )

    def swap(part, distance):
        return lax.ppermute(part, "stream", [(i, i ^ distance) for i in range(streams)])

    got = [piece0, swap(piece1, 1), swap(piece2, 2), swap(piece3, 3)]
    pick = lambda parts, j: functools.reduce(
        lambda rest, k: jnp.where((member ^ k) == j, parts[k], rest), range(1, GROUP), parts[0]
    )
    ordered = [pick(got, j).astype(F32) for j in range(GROUP)]
    values = [part[:piece] for part in ordered]
    factors = [part[piece : piece + 1] + part[piece + 1 : piece + 2] for part in ordered]

    total, total_factor = values[0], factors[0]
    for j in range(1, GROUP):
        total = factors[j] * total + values[j]
        total_factor = total_factor * factors[j]
    before, before_factor = jnp.zeros_like(total), jnp.ones_like(total_factor)
    distance = GROUP
    while distance < streams:
        last = 2 * distance >= streams
        if last:
            met = swap(total.astype(BF16), distance).astype(F32)
        else:
            high = total_factor.astype(BF16)
            low = (total_factor - high.astype(F32)).astype(BF16)
            met = swap(jnp.concatenate([total.astype(BF16), high, low], axis=0), distance).astype(F32)
        later = (stream & distance) != 0
        before = jnp.where(later, before_factor * met[:piece] + before, before)
        if not last:
            met_factor = met[piece : piece + 1] + met[piece + 1 : piece + 2]
            before_factor = jnp.where(later, before_factor * met_factor, before_factor)
            total = jnp.where(later, total_factor * met[:piece] + total, met_factor * total + met[:piece])
            total_factor = total_factor * met_factor
        distance *= 2

    entering = [before]
    for j in range(GROUP - 1):
        entering.append(factors[j] * entering[j] + values[j])
    entering = [part.astype(BF16) for part in entering]
    give = [pick(entering, k) for k in range(GROUP)]
    back = [give[0]] + [swap(give[k], k) for k in range(1, GROUP)]

    return call(
        final_kernel,
        place,
        (far, near, retention, *back[::-1]),
        [vmem] * (3 + GROUP),
        like(cells.shape, F32),
        hbm,
        [pltpu.VMEM((2 * width, dofs), F32), pltpu.VMEM(cells.shape, F32), pltpu.SemaphoreType.DMA((layers,))],
        1_000_000,
        4_000_000,
    )


def solution(mesh):
    return jax.shard_map(
        body,
        mesh=mesh,
        in_specs=(
            P("stream", "cross", None, None),
            P("stream", "cross", None, None),
            P(None, "stream", "cross", None),
            P(),
            P("stream", "cross", None, None),
            P("stream", None),
        ),
        out_specs=P("stream", "cross", None, None),
        check_vma=False,
    )
```

```python
import functools

import jax
import jax.numpy as jnp
from jax import lax
from jax.experimental import pallas as pl
from jax.experimental.pallas import tpu as pltpu
from jax.sharding import PartitionSpec as P

GROUP = 4
F32, BF16 = jnp.float32, jnp.bfloat16
VMEM_LIMIT = 24 * 1024 * 1024
MASK_COST = 10_000_000_000


def masked_jump(mask, neighbour, center):
    return (mask * (neighbour - center)).astype(BF16)


def along_b(cells):
    rows = lax.broadcasted_iota(jnp.int32, cells.shape, 0)
    last = cells.shape[0] - 1
    lower = jnp.where(rows == 0, 0.0, pltpu.roll(cells, 1, 0))
    upper = jnp.where(rows == last, 0.0, pltpu.roll(cells, last, 0))
    return lower, upper


def mask_columns(mask_ref, layer):
    rows = [mask_ref[face, layer, a : a + 1, :] for face in range(4) for a in range(2)]
    rows.append(jnp.zeros((120, rows[0].shape[1]), rows[0].dtype))
    return jnp.concatenate(rows, axis=0).astype(F32).T


def dot(a, b):
    return jnp.dot(a, b, preferred_element_type=F32)


def mask_kernel(mask_ref, after, columns_ref):
    for l in range(columns_ref.shape[0]):
        columns_ref[l] = mask_columns(mask_ref, l)


def inner_kernel(columns_ref, halo_ref, keep_ref, near_row, far_row, forcing, lift, inverse, far_ref, source_ref, jumps):
    layers, width, dofs = near_row.shape
    odd = lax.axis_index("cross") & 1
    near_at, far_at = odd, 1 - odd
    is_odd = odd == 1
    outward = pl.ds(pl.multiple_of((1 - odd) * dofs, 128), dofs)
    inward = pl.ds(pl.multiple_of(odd * dofs, 128), dofs)
    weights = lift[...].reshape(4 * dofs, dofs)
    carry = None
    for l in range(layers):
        columns = columns_ref[l]
        column = lambda face, even, other: jnp.where(
            is_odd, columns[:, 2 * face[1] + other : 2 * face[1] + other + 1], columns[:, 2 * face[0] + even : 2 * face[0] + even + 1]
        )
        near, far = near_row[l].astype(F32), far_row[l].astype(F32)
        far_at_rows = pl.ds(2 * l * width, width)
        near_at_rows = pl.ds((2 * l + 1) * width, width)
        step = near - far
        jumps[far_at_rows, outward] = masked_jump(column((1, 0), 1, 0), halo_ref[l].astype(F32), far)
        jumps[far_at_rows, inward] = (column((0, 1), 1, 0) * step).astype(BF16)
        jumps[near_at_rows, outward] = (column((1, 0), 0, 1) * -step).astype(BF16)
        jumps[near_at_rows, inward] = jnp.zeros((width, dofs), BF16)
        for at, cells, even in ((far_at_rows, far, 1), (near_at_rows, near, 0)):
            low, up = along_b(cells)
            jumps[at, pl.ds(2 * dofs, dofs)] = masked_jump(column((2, 2), even, 1 - even), low, cells)
            jumps[at, pl.ds(3 * dofs, dofs)] = masked_jump(column((3, 3), even, 1 - even), up, cells)
        lifted = dot(jumps[pl.ds(2 * l * width, 2 * width), :], weights)
        source_ref[l] = forcing[l, near_at].astype(F32) + lifted[width:]
        far_source = forcing[l, far_at].astype(F32) + lifted[:width]
        solved = dot(far_source.astype(BF16), inverse[l, far_at])
        carry = solved if l == 0 else keep_ref[l : l + 1, :] * carry + solved
        far_ref[l] = carry


def outer_kernel(halo_ref, columns_ref, near_row, source_ref, lift, inverse, keep_ref, far_ref, near_ref, p0, p3, p2, p1, carry):
    layers, width, dofs = near_row.shape
    odd = lax.axis_index("cross") & 1
    cross = lax.axis_index("cross")
    inside = (cross != 0) & (cross != lax.axis_size("cross") - 1)
    jumps = []
    for l in range(layers):
        edge = jnp.where(odd == 1, columns_ref[l, :, 3:4], columns_ref[l, :, 0:1])
        halo = jnp.where(inside, halo_ref[l].astype(F32), 0.0)
        jumps.append(masked_jump(edge, halo, near_row[l].astype(F32)))
    lifted = dot(jnp.concatenate(jumps, axis=0), lift[odd])
    total = None
    for l in range(layers):
        source = source_ref[l] + lifted[l * width : (l + 1) * width]
        solved = dot(source.astype(BF16), inverse[l, odd])
        total = solved if l == 0 else keep_ref[l : l + 1, :] * total + solved
        near_ref[l] = total
    carry[pl.ds(0, width), :] = far_ref[layers - 1]
    carry[pl.ds(width, width), :] = total
    factor = keep_ref[0:1, :]
    for l in range(1, layers):
        factor = factor * keep_ref[l : l + 1, :]
    high = factor.astype(BF16).astype(F32)
    low = factor - high
    at = lax.broadcasted_iota(jnp.int32, (8, dofs), 0)
    extra = jnp.where(at == 0, high, jnp.where(at == 1, low, 0.0))
    piece = 2 * width // GROUP
    member = lax.axis_index("stream") & (GROUP - 1)
    for k, out in enumerate((p0, p1, p2, p3)):
        start = pl.multiple_of((member ^ k) * piece, 8)
        out[...] = jnp.concatenate([carry[pl.ds(start, piece), :], extra], axis=0).astype(BF16)


def final_kernel(far_ref, near_ref, keep_ref, e3, e2, e1, e0, out_hbm, incoming, out, sem):
    layers, width, dofs = far_ref.shape
    odd = lax.axis_index("cross") & 1
    piece = e0.shape[0]
    member = lax.axis_index("stream") & (GROUP - 1)
    for k, part in enumerate((e0, e1, e2, e3)):
        start = pl.multiple_of((member ^ k) * piece, 8)
        incoming[pl.ds(start, piece), :] = part[...].astype(F32)
    copies = []
    factor = None
    for l in range(layers):
        factor = keep_ref[l : l + 1, :] if l == 0 else factor * keep_ref[l : l + 1, :]
        out[l, 1 - odd] = far_ref[l] + factor * incoming[pl.ds(0, width), :]
        out[l, odd] = near_ref[l] + factor * incoming[pl.ds(width, width), :]
        copies.append(pltpu.make_async_copy(out.at[l], out_hbm.at[l], sem.at[l]))
        copies[-1].start()
    for copy in copies:
        copy.wait()


def call(kernel, operands, in_specs, outs, out_specs, scratch, flops, moved):
    return pl.pallas_call(
        kernel,
        out_shape=outs,
        in_specs=in_specs,
        out_specs=out_specs,
        scratch_shapes=scratch,
        compiler_params=pltpu.CompilerParams(vmem_limit_bytes=VMEM_LIMIT),
        cost_estimate=pl.CostEstimate(flops=flops, bytes_accessed=moved, transcendentals=0),
    )(*operands)


def body(forcing, cells, face_mask, lifting, inverse, retention):
    layers, _, width, dofs = cells.shape
    crosses, streams = lax.axis_size("cross"), lax.axis_size("stream")
    cross, stream = lax.axis_index("cross"), lax.axis_index("stream")
    odd, member = cross % 2, stream % GROUP

    links = []
    for s in range(streams):
        for c in range(crosses):
            other = (s ^ 1, c) if c in (0, crosses - 1) else (s, c + 1 if c % 2 else c - 1)
            links.append((s * crosses + c, other[0] * crosses + other[1]))
    vmem, hbm = pl.BlockSpec(memory_space=pltpu.VMEM), pl.BlockSpec(memory_space=pl.ANY)
    like = jax.ShapeDtypeStruct
    stack = like((layers, width, dofs), F32)
    slab = like((layers, width, dofs), BF16)
    unit = 2 * layers * width * dofs * dofs

    near_row = lax.dynamic_index_in_dim(cells, odd, 1, False)
    far_row = lax.dynamic_index_in_dim(lax.optimization_barrier(cells), 1 - odd, 1, False)
    chip_halo = lax.ppermute(near_row, ("stream", "cross"), links)
    core_halo = lax.ppermute(far_row, "cross", [(i, i ^ 1) for i in range(crosses)])
    columns = call(
        mask_kernel, (face_mask, near_row), [vmem, hbm], like((layers, width, 128), F32), vmem, [], MASK_COST, 20_000_000
    )
    far, near_source = call(
        inner_kernel,
        (columns, core_halo, retention, near_row, far_row, forcing, lifting, inverse),
        [vmem] * 8,
        (stack, stack),
        (vmem,) * 2,
        [pltpu.VMEM((2 * layers * width, 4 * dofs), BF16)],
        9 * unit,
        5_000_000,
    )

    piece = 2 * width // GROUP
    near, piece0, piece3, piece2, piece1 = call(
        outer_kernel,
        (chip_halo, columns, near_row, near_source, lifting, inverse, retention, far),
        [vmem] * 8,
        (stack,) + (like((piece + 8, dofs), BF16),) * GROUP,
        (vmem,) * (1 + GROUP),
        [pltpu.VMEM((2 * width, dofs), F32)],
        2 * unit,
        3_000_000,
    )

    def swap(part, distance):
        return lax.ppermute(part, "stream", [(i, i ^ distance) for i in range(streams)])

    got = [piece0, swap(piece1, 1), swap(piece2, 2), swap(piece3, 3)]
    pick = lambda parts, j: functools.reduce(
        lambda rest, k: jnp.where((member ^ k) == j, parts[k], rest), range(1, GROUP), parts[0]
    )
    ordered = [pick(got, j).astype(F32) for j in range(GROUP)]
    values = [part[:piece] for part in ordered]
    factors = [part[piece : piece + 1] + part[piece + 1 : piece + 2] for part in ordered]

    total, total_factor = values[0], factors[0]
    for j in range(1, GROUP):
        total = factors[j] * total + values[j]
        total_factor = total_factor * factors[j]
    before, before_factor = jnp.zeros_like(total), jnp.ones_like(total_factor)
    distance = GROUP
    while distance < streams:
        last = 2 * distance >= streams
        if last:
            met = swap(total.astype(BF16), distance).astype(F32)
        else:
            high = total_factor.astype(BF16)
            low = (total_factor - high.astype(F32)).astype(BF16)
            met = swap(jnp.concatenate([total.astype(BF16), high, low], axis=0), distance).astype(F32)
        later = (stream & distance) != 0
        before = jnp.where(later, before_factor * met[:piece] + before, before)
        if not last:
            met_factor = met[piece : piece + 1] + met[piece + 1 : piece + 2]
            before_factor = jnp.where(later, before_factor * met_factor, before_factor)
            total = jnp.where(later, total_factor * met[:piece] + total, met_factor * total + met[:piece])
            total_factor = total_factor * met_factor
        distance *= 2

    entering = [before]
    for j in range(GROUP - 1):
        entering.append(factors[j] * entering[j] + values[j])
    entering = [part.astype(BF16) for part in entering]
    give = [pick(entering, k) for k in range(GROUP)]
    back = [give[0]] + [swap(give[k], k) for k in range(1, GROUP)]

    return call(
        final_kernel,
        (far, near, retention, *back[::-1]),
        [vmem] * (3 + GROUP),
        like(cells.shape, F32),
        hbm,
        [pltpu.VMEM((2 * width, dofs), F32), pltpu.VMEM(cells.shape, F32), pltpu.SemaphoreType.DMA((layers,))],
        1_000_000,
        4_000_000,
    )


def solution(mesh):
    return jax.shard_map(
        body,
        mesh=mesh,
        in_specs=(
            P("stream", "cross", None, None),
            P("stream", "cross", None, None),
            P(None, "stream", "cross", None),
            P(),
            P("stream", "cross", None, None),
            P("stream", None),
        ),
        out_specs=P("stream", "cross", None, None),
        check_vma=False,
    )
```

```python
import functools

import jax
import jax.numpy as jnp
from jax import lax
from jax.experimental import pallas as pl
from jax.experimental.pallas import tpu as pltpu
from jax.sharding import PartitionSpec as P

GROUP = 4
F32, BF16 = jnp.float32, jnp.bfloat16
VMEM_LIMIT = 24 * 1024 * 1024
MASK_COST = 10_000_000_000


def masked_jump(mask, neighbour, center):
    return (mask * (neighbour - center)).astype(BF16)


def along_b(cells):
    rows = lax.broadcasted_iota(jnp.int32, cells.shape, 0)
    last = cells.shape[0] - 1
    lower = jnp.where(rows == 0, 0.0, pltpu.roll(cells, 1, 0))
    upper = jnp.where(rows == last, 0.0, pltpu.roll(cells, last, 0))
    return lower, upper


def mask_columns(mask_ref, layer):
    rows = [mask_ref[face, layer, a : a + 1, :] for face in range(4) for a in range(2)]
    rows.append(jnp.zeros((120, rows[0].shape[1]), rows[0].dtype))
    return jnp.concatenate(rows, axis=0).astype(F32).T


def dot(a, b):
    return jnp.dot(a, b, preferred_element_type=F32)


def mask_kernel(mask_ref, after, columns_ref):
    for l in range(columns_ref.shape[0]):
        columns_ref[l] = mask_columns(mask_ref, l)


def inner_kernel(columns_ref, halo_ref, keep_ref, near_row, far_row, forcing, lift, inverse, far_ref, start_ref, matrix_ref, jumps):
    layers, width, dofs = near_row.shape
    odd = lax.axis_index("cross") & 1
    near_at, far_at = odd, 1 - odd
    is_odd = odd == 1
    outward = pl.ds(pl.multiple_of((1 - odd) * dofs, 128), dofs)
    inward = pl.ds(pl.multiple_of(odd * dofs, 128), dofs)
    weights = lift[...].reshape(4 * dofs, dofs)
    far_carry = near_carry = None
    for l in range(layers):
        columns = columns_ref[l]
        column = lambda face, even, other: jnp.where(
            is_odd, columns[:, 2 * face[1] + other : 2 * face[1] + other + 1], columns[:, 2 * face[0] + even : 2 * face[0] + even + 1]
        )
        near, far = near_row[l].astype(F32), far_row[l].astype(F32)
        far_at_rows = pl.ds(2 * l * width, width)
        near_at_rows = pl.ds((2 * l + 1) * width, width)
        step = near - far
        jumps[far_at_rows, outward] = masked_jump(column((1, 0), 1, 0), halo_ref[l].astype(F32), far)
        jumps[far_at_rows, inward] = (column((0, 1), 1, 0) * step).astype(BF16)
        jumps[near_at_rows, outward] = (column((1, 0), 0, 1) * -step).astype(BF16)
        jumps[near_at_rows, inward] = jnp.zeros((width, dofs), BF16)
        for at, cells, even in ((far_at_rows, far, 1), (near_at_rows, near, 0)):
            low, up = along_b(cells)
            jumps[at, pl.ds(2 * dofs, dofs)] = masked_jump(column((2, 2), even, 1 - even), low, cells)
            jumps[at, pl.ds(3 * dofs, dofs)] = masked_jump(column((3, 3), even, 1 - even), up, cells)
        lifted = dot(jumps[pl.ds(2 * l * width, 2 * width), :], weights)
        near_source = forcing[l, near_at].astype(F32) + lifted[width:]
        far_source = forcing[l, far_at].astype(F32) + lifted[:width]
        near_solved = dot(near_source.astype(BF16), inverse[l, near_at])
        far_solved = dot(far_source.astype(BF16), inverse[l, far_at])
        matrix_ref[l] = dot(lift[odd], inverse[l, near_at]).astype(BF16)
        far_carry = far_solved if l == 0 else keep_ref[l : l + 1, :] * far_carry + far_solved
        near_carry = near_solved if l == 0 else keep_ref[l : l + 1, :] * near_carry + near_solved
        far_ref[l] = far_carry
        start_ref[l] = near_carry


def outer_kernel(halo_ref, columns_ref, near_row, start_ref, matrix_ref, keep_ref, far_ref, near_ref, p0, p3, p2, p1, carry):
    layers, width, dofs = near_row.shape
    cross = lax.axis_index("cross")
    odd = cross & 1
    inside = (cross != 0) & (cross != lax.axis_size("cross") - 1)
    total = None
    for l in range(layers):
        edge = jnp.where(odd == 1, columns_ref[l, :, 3:4], columns_ref[l, :, 0:1])
        halo = jnp.where(inside, halo_ref[l].astype(F32), 0.0)
        solved = dot(masked_jump(edge, halo, near_row[l].astype(F32)), matrix_ref[l])
        total = solved if l == 0 else keep_ref[l : l + 1, :] * total + solved
        near_ref[l] = start_ref[l] + total
    total = total + start_ref[layers - 1]
    carry[pl.ds(0, width), :] = far_ref[layers - 1]
    carry[pl.ds(width, width), :] = total
    factor = keep_ref[0:1, :]
    for l in range(1, layers):
        factor = factor * keep_ref[l : l + 1, :]
    high = factor.astype(BF16).astype(F32)
    low = factor - high
    at = lax.broadcasted_iota(jnp.int32, (8, dofs), 0)
    extra = jnp.where(at == 0, high, jnp.where(at == 1, low, 0.0))
    piece = 2 * width // GROUP
    member = lax.axis_index("stream") & (GROUP - 1)
    for k, out in enumerate((p0, p1, p2, p3)):
        start = pl.multiple_of((member ^ k) * piece, 8)
        out[...] = jnp.concatenate([carry[pl.ds(start, piece), :], extra], axis=0).astype(BF16)


def final_kernel(far_ref, near_ref, keep_ref, e3, e2, e1, e0, out_hbm, incoming, out, sem):
    layers, width, dofs = far_ref.shape
    odd = lax.axis_index("cross") & 1
    piece = e0.shape[0]
    member = lax.axis_index("stream") & (GROUP - 1)
    for k, part in enumerate((e0, e1, e2, e3)):
        start = pl.multiple_of((member ^ k) * piece, 8)
        incoming[pl.ds(start, piece), :] = part[...].astype(F32)
    copies = []
    factor = None
    for l in range(layers):
        factor = keep_ref[l : l + 1, :] if l == 0 else factor * keep_ref[l : l + 1, :]
        out[l, 1 - odd] = far_ref[l] + factor * incoming[pl.ds(0, width), :]
        out[l, odd] = near_ref[l] + factor * incoming[pl.ds(width, width), :]
        copies.append(pltpu.make_async_copy(out.at[l], out_hbm.at[l], sem.at[l]))
        copies[-1].start()
    for copy in copies:
        copy.wait()


def call(kernel, operands, in_specs, outs, out_specs, scratch, flops, moved):
    return pl.pallas_call(
        kernel,
        out_shape=outs,
        in_specs=in_specs,
        out_specs=out_specs,
        scratch_shapes=scratch,
        compiler_params=pltpu.CompilerParams(vmem_limit_bytes=VMEM_LIMIT),
        cost_estimate=pl.CostEstimate(flops=flops, bytes_accessed=moved, transcendentals=0),
    )(*operands)


def body(forcing, cells, face_mask, lifting, inverse, retention):
    layers, _, width, dofs = cells.shape
    crosses, streams = lax.axis_size("cross"), lax.axis_size("stream")
    cross, stream = lax.axis_index("cross"), lax.axis_index("stream")
    odd, member = cross % 2, stream % GROUP

    links = []
    for s in range(streams):
        for c in range(crosses):
            other = (s ^ 1, c) if c in (0, crosses - 1) else (s, c + 1 if c % 2 else c - 1)
            links.append((s * crosses + c, other[0] * crosses + other[1]))
    vmem, hbm = pl.BlockSpec(memory_space=pltpu.VMEM), pl.BlockSpec(memory_space=pl.ANY)
    like = jax.ShapeDtypeStruct
    stack = like((layers, width, dofs), F32)
    slab = like((layers, width, dofs), BF16)
    unit = 2 * layers * width * dofs * dofs

    near_row = lax.dynamic_index_in_dim(cells, odd, 1, False)
    far_row = lax.dynamic_index_in_dim(lax.optimization_barrier((cells, near_row))[0], 1 - odd, 1, False)
    chip_halo = lax.ppermute(near_row, ("stream", "cross"), links)
    core_halo = lax.ppermute(far_row, "cross", [(i, i ^ 1) for i in range(crosses)])
    columns = call(
        mask_kernel, (face_mask, near_row), [vmem, hbm], like((layers, width, 128), F32), vmem, [], MASK_COST, 20_000_000
    )
    far, near_start, matrix = call(
        inner_kernel,
        (columns, core_halo, retention, near_row, far_row, forcing, lifting, inverse),
        [vmem] * 8,
        (stack, stack, like((layers, dofs, dofs), BF16)),
        (vmem,) * 3,
        [pltpu.VMEM((2 * layers * width, 4 * dofs), BF16)],
        9 * unit,
        5_000_000,
    )

    piece = 2 * width // GROUP
    near, piece0, piece3, piece2, piece1 = call(
        outer_kernel,
        (chip_halo, columns, near_row, near_start, matrix, retention, far),
        [vmem] * 7,
        (stack,) + (like((piece + 8, dofs), BF16),) * GROUP,
        (vmem,) * (1 + GROUP),
        [pltpu.VMEM((2 * width, dofs), F32)],
        2 * unit,
        3_000_000,
    )

    def swap(part, distance):
        return lax.ppermute(part, "stream", [(i, i ^ distance) for i in range(streams)])

    got = [piece0, swap(piece1, 1), swap(piece2, 2), swap(piece3, 3)]
    pick = lambda parts, j: functools.reduce(
        lambda rest, k: jnp.where((member ^ k) == j, parts[k], rest), range(1, GROUP), parts[0]
    )
    ordered = [pick(got, j).astype(F32) for j in range(GROUP)]
    values = [part[:piece] for part in ordered]
    factors = [part[piece : piece + 1] + part[piece + 1 : piece + 2] for part in ordered]

    total, total_factor = values[0], factors[0]
    for j in range(1, GROUP):
        total = factors[j] * total + values[j]
        total_factor = total_factor * factors[j]
    before, before_factor = jnp.zeros_like(total), jnp.ones_like(total_factor)
    distance = GROUP
    while distance < streams:
        last = 2 * distance >= streams
        if last:
            met = swap(total.astype(BF16), distance).astype(F32)
        else:
            high = total_factor.astype(BF16)
            low = (total_factor - high.astype(F32)).astype(BF16)
            met = swap(jnp.concatenate([total.astype(BF16), high, low], axis=0), distance).astype(F32)
        later = (stream & distance) != 0
        before = jnp.where(later, before_factor * met[:piece] + before, before)
        if not last:
            met_factor = met[piece : piece + 1] + met[piece + 1 : piece + 2]
            before_factor = jnp.where(later, before_factor * met_factor, before_factor)
            total = jnp.where(later, total_factor * met[:piece] + total, met_factor * total + met[:piece])
            total_factor = total_factor * met_factor
        distance *= 2

    entering = [before]
    for j in range(GROUP - 1):
        entering.append(factors[j] * entering[j] + values[j])
    entering = [part.astype(BF16) for part in entering]
    give = [pick(entering, k) for k in range(GROUP)]
    back = [give[0]] + [swap(give[k], k) for k in range(1, GROUP)]

    return call(
        final_kernel,
        (far, near, retention, *back[::-1]),
        [vmem] * (3 + GROUP),
        like(cells.shape, F32),
        hbm,
        [pltpu.VMEM((2 * width, dofs), F32), pltpu.VMEM(cells.shape, F32), pltpu.SemaphoreType.DMA((layers,))],
        1_000_000,
        4_000_000,
    )


def solution(mesh):
    return jax.shard_map(
        body,
        mesh=mesh,
        in_specs=(
            P("stream", "cross", None, None),
            P("stream", "cross", None, None),
            P(None, "stream", "cross", None),
            P(),
            P("stream", "cross", None, None),
            P("stream", None),
        ),
        out_specs=P("stream", "cross", None, None),
        check_vma=False,
    )
```

```python
import functools

import jax
import jax.numpy as jnp
from jax import lax
from jax.experimental import pallas as pl
from jax.experimental.pallas import tpu as pltpu
from jax.sharding import PartitionSpec as P

GROUP = 4
F32, BF16 = jnp.float32, jnp.bfloat16
VMEM_LIMIT = 24 * 1024 * 1024
MASK_COST = 10_000_000_000


def masked_jump(mask, neighbour, center):
    return (mask * (neighbour - center)).astype(BF16)


def along_b(cells):
    rows = lax.broadcasted_iota(jnp.int32, cells.shape, 0)
    last = cells.shape[0] - 1
    lower = jnp.where(rows == 0, 0.0, pltpu.roll(cells, 1, 0))
    upper = jnp.where(rows == last, 0.0, pltpu.roll(cells, last, 0))
    return lower, upper


def mask_columns(mask_ref, layer):
    rows = [mask_ref[face, layer, a : a + 1, :] for face in range(4) for a in range(2)]
    rows.append(jnp.zeros((120, rows[0].shape[1]), rows[0].dtype))
    return jnp.concatenate(rows, axis=0).astype(F32).T


def dot(a, b):
    return jnp.dot(a, b, preferred_element_type=F32)


def mask_kernel(mask_ref, after, columns_ref):
    for l in range(columns_ref.shape[0]):
        columns_ref[l] = mask_columns(mask_ref, l)


def inner_kernel(columns_ref, halo_ref, keep_ref, near_row, far_row, forcing, lift, inverse, far_ref, start_ref, matrix_ref, jumps):
    layers, width, dofs = near_row.shape
    odd = lax.axis_index("cross") & 1
    near_at, far_at = odd, 1 - odd
    is_odd = odd == 1
    outward = pl.ds(pl.multiple_of((1 - odd) * dofs, 128), dofs)
    inward = pl.ds(pl.multiple_of(odd * dofs, 128), dofs)
    weights = lift[...].reshape(4 * dofs, dofs)
    far_carry = near_carry = None
    for l in range(layers):
        columns = columns_ref[l]
        column = lambda face, even, other: jnp.where(
            is_odd, columns[:, 2 * face[1] + other : 2 * face[1] + other + 1], columns[:, 2 * face[0] + even : 2 * face[0] + even + 1]
        )
        near, far = near_row[l].astype(F32), far_row[l].astype(F32)
        far_at_rows = pl.ds(2 * l * width, width)
        near_at_rows = pl.ds((2 * l + 1) * width, width)
        step = near - far
        jumps[far_at_rows, outward] = masked_jump(column((1, 0), 1, 0), halo_ref[l].astype(F32), far)
        jumps[far_at_rows, inward] = (column((0, 1), 1, 0) * step).astype(BF16)
        jumps[near_at_rows, outward] = (column((1, 0), 0, 1) * -step).astype(BF16)
        jumps[near_at_rows, inward] = jnp.zeros((width, dofs), BF16)
        for at, cells, even in ((far_at_rows, far, 1), (near_at_rows, near, 0)):
            low, up = along_b(cells)
            jumps[at, pl.ds(2 * dofs, dofs)] = masked_jump(column((2, 2), even, 1 - even), low, cells)
            jumps[at, pl.ds(3 * dofs, dofs)] = masked_jump(column((3, 3), even, 1 - even), up, cells)
        lifted = dot(jumps[pl.ds(2 * l * width, 2 * width), :], weights)
        near_source = forcing[l, near_at].astype(F32) + lifted[width:]
        far_source = forcing[l, far_at].astype(F32) + lifted[:width]
        near_solved = dot(near_source.astype(BF16), inverse[l, near_at])
        far_solved = dot(far_source.astype(BF16), inverse[l, far_at])
        matrix_ref[l] = dot(lift[odd], inverse[l, near_at]).astype(BF16)
        far_carry = far_solved if l == 0 else keep_ref[l : l + 1, :] * far_carry + far_solved
        near_carry = near_solved if l == 0 else keep_ref[l : l + 1, :] * near_carry + near_solved
        far_ref[l] = far_carry
        start_ref[l] = near_carry


def outer_kernel(halo_ref, columns_ref, near_row, start_ref, matrix_ref, keep_ref, far_ref, near_ref, p0, p3, p2, p1, carry):
    layers, width, dofs = near_row.shape
    cross = lax.axis_index("cross")
    odd = cross & 1
    inside = (cross != 0) & (cross != lax.axis_size("cross") - 1)
    total = None
    for l in range(layers):
        edge = jnp.where(odd == 1, columns_ref[l, :, 3:4], columns_ref[l, :, 0:1])
        halo = jnp.where(inside, halo_ref[l].astype(F32), 0.0)
        solved = dot(masked_jump(edge, halo, near_row[l].astype(F32)), matrix_ref[l])
        total = solved if l == 0 else keep_ref[l : l + 1, :] * total + solved
        near_ref[l] = start_ref[l] + total
    total = total + start_ref[layers - 1]
    carry[pl.ds(0, width), :] = far_ref[layers - 1]
    carry[pl.ds(width, width), :] = total
    factor = keep_ref[0:1, :]
    for l in range(1, layers):
        factor = factor * keep_ref[l : l + 1, :]
    high = factor.astype(BF16).astype(F32)
    low = factor - high
    at = lax.broadcasted_iota(jnp.int32, (8, dofs), 0)
    extra = jnp.where(at == 0, high, jnp.where(at == 1, low, 0.0))
    piece = 2 * width // GROUP
    member = lax.axis_index("stream") & (GROUP - 1)
    for k, out in enumerate((p0, p1, p2, p3)):
        start = pl.multiple_of((member ^ k) * piece, 8)
        out[...] = jnp.concatenate([carry[pl.ds(start, piece), :], extra], axis=0).astype(BF16)


def final_kernel(far_ref, near_ref, keep_ref, e3, e2, e1, e0, out_hbm, incoming, out, sem):
    layers, width, dofs = far_ref.shape
    odd = lax.axis_index("cross") & 1
    piece = e0.shape[0]
    member = lax.axis_index("stream") & (GROUP - 1)
    for k, part in enumerate((e0, e1, e2, e3)):
        start = pl.multiple_of((member ^ k) * piece, 8)
        incoming[pl.ds(start, piece), :] = part[...].astype(F32)
    copies = []
    factor = None
    for l in range(layers):
        factor = keep_ref[l : l + 1, :] if l == 0 else factor * keep_ref[l : l + 1, :]
        out[l, 1 - odd] = far_ref[l] + factor * incoming[pl.ds(0, width), :]
        out[l, odd] = near_ref[l] + factor * incoming[pl.ds(width, width), :]
        copies.append(pltpu.make_async_copy(out.at[l], out_hbm.at[l], sem.at[l]))
        copies[-1].start()
    for copy in copies:
        copy.wait()


def call(kernel, operands, in_specs, outs, out_specs, scratch, flops, moved):
    return pl.pallas_call(
        kernel,
        out_shape=outs,
        in_specs=in_specs,
        out_specs=out_specs,
        scratch_shapes=scratch,
        compiler_params=pltpu.CompilerParams(vmem_limit_bytes=VMEM_LIMIT),
        cost_estimate=pl.CostEstimate(flops=flops, bytes_accessed=moved, transcendentals=0),
    )(*operands)


def body(forcing, cells, face_mask, lifting, inverse, retention):
    layers, _, width, dofs = cells.shape
    crosses, streams = lax.axis_size("cross"), lax.axis_size("stream")
    cross, stream = lax.axis_index("cross"), lax.axis_index("stream")
    odd, member = cross % 2, stream % GROUP

    links = []
    for s in range(streams):
        for c in range(crosses):
            other = (s ^ 1, c) if c in (0, crosses - 1) else (s, c + 1 if c % 2 else c - 1)
            links.append((s * crosses + c, other[0] * crosses + other[1]))
    vmem, hbm = pl.BlockSpec(memory_space=pltpu.VMEM), pl.BlockSpec(memory_space=pl.ANY)
    like = jax.ShapeDtypeStruct
    stack = like((layers, width, dofs), F32)
    slab = like((layers, width, dofs), BF16)
    unit = 2 * layers * width * dofs * dofs

    near_row = lax.dynamic_index_in_dim(cells, odd, 1, False)
    far_row = lax.dynamic_index_in_dim(lax.optimization_barrier((cells, near_row))[0], 1 - odd, 1, False)
    chip_halo = lax.ppermute(near_row, ("stream", "cross"), links)
    core_halo = lax.ppermute(far_row, "cross", [(i, i ^ 1) for i in range(crosses)])
    columns = call(
        mask_kernel, (face_mask, near_row), [vmem, hbm], like((layers, width, 128), F32), vmem, [], MASK_COST, 20_000_000
    )
    far, near_start, matrix = call(
        inner_kernel,
        (columns, core_halo, retention, near_row, far_row, forcing, lifting, inverse),
        [vmem] * 8,
        (stack, stack, like((layers, dofs, dofs), BF16)),
        (vmem,) * 3,
        [pltpu.VMEM((2 * layers * width, 4 * dofs), BF16)],
        9 * unit,
        5_000_000,
    )

    piece = 2 * width // GROUP
    near, piece0, piece3, piece2, piece1 = call(
        outer_kernel,
        (chip_halo, columns, near_row, near_start, matrix, retention, far),
        [vmem] * 7,
        (stack,) + (like((piece + 8, dofs), BF16),) * GROUP,
        (vmem,) * (1 + GROUP),
        [pltpu.VMEM((2 * width, dofs), F32)],
        2 * unit,
        3_000_000,
    )

    def swap(part, distance):
        return lax.ppermute(part, "stream", [(i, i ^ distance) for i in range(streams)])

    got = [piece0, swap(piece1, 1), swap(piece2, 2), swap(piece3, 3)]
    pick = lambda parts, j: functools.reduce(
        lambda rest, k: jnp.where((member ^ k) == j, parts[k], rest), range(1, GROUP), parts[0]
    )
    ordered = [pick(got, j).astype(F32) for j in range(GROUP)]
    values = [part[:piece] for part in ordered]
    factors = [part[piece : piece + 1] + part[piece + 1 : piece + 2] for part in ordered]

    total, total_factor = values[0], factors[0]
    for j in range(1, GROUP):
        total = factors[j] * total + values[j]
        total_factor = total_factor * factors[j]
    before, before_factor = jnp.zeros_like(total), jnp.ones_like(total_factor)
    distance = GROUP
    while distance < streams:
        later = (stream & distance) != 0
        if streams == 2 * GROUP:
            before = jnp.where(later, swap(total.astype(BF16), distance).astype(F32), before)
        else:
            met = swap(jnp.concatenate([total, total_factor], axis=0), distance)
            met, met_factor = met[:piece], met[piece:]
            before = jnp.where(later, before_factor * met + before, before)
            before_factor = jnp.where(later, before_factor * met_factor, before_factor)
            total = jnp.where(later, total_factor * met + total, met_factor * total + met)
            total_factor = total_factor * met_factor
        distance *= 2

    entering = [before]
    for j in range(GROUP - 1):
        entering.append(factors[j] * entering[j] + values[j])
    entering = [part.astype(BF16) for part in entering]
    give = [pick(entering, k) for k in range(GROUP)]
    back = [give[0]] + [swap(give[k], k) for k in range(1, GROUP)]

    return call(
        final_kernel,
        (far, near, retention, *back[::-1]),
        [vmem] * (3 + GROUP),
        like(cells.shape, F32),
        hbm,
        [pltpu.VMEM((2 * width, dofs), F32), pltpu.VMEM(cells.shape, F32), pltpu.SemaphoreType.DMA((layers,))],
        1_000_000,
        4_000_000,
    )


def solution(mesh):
    return jax.shard_map(
        body,
        mesh=mesh,
        in_specs=(
            P("stream", "cross", None, None),
            P("stream", "cross", None, None),
            P(None, "stream", "cross", None),
            P(),
            P("stream", "cross", None, None),
            P("stream", None),
        ),
        out_specs=P("stream", "cross", None, None),
        check_vma=False,
    )
```

```python
import functools

import jax
import jax.numpy as jnp
from jax import lax
from jax.experimental import pallas as pl
from jax.experimental.pallas import tpu as pltpu
from jax.sharding import PartitionSpec as P

GROUP = 4
F32, BF16 = jnp.float32, jnp.bfloat16
VMEM_LIMIT = 24 * 1024 * 1024
MASK_COST = 10_000_000_000


def masked_jump(mask, neighbour, center):
    return (mask * (neighbour - center)).astype(BF16)


def along_b(cells):
    rows = lax.broadcasted_iota(jnp.int32, cells.shape, 0)
    last = cells.shape[0] - 1
    lower = jnp.where(rows == 0, 0.0, pltpu.roll(cells, 1, 0))
    upper = jnp.where(rows == last, 0.0, pltpu.roll(cells, last, 0))
    return lower, upper


def mask_columns(mask_ref, layer):
    rows = [mask_ref[face, layer, a : a + 1, :] for face in range(4) for a in range(2)]
    rows.append(jnp.zeros((120, rows[0].shape[1]), rows[0].dtype))
    return jnp.concatenate(rows, axis=0).astype(F32).T


def dot(a, b):
    return jnp.dot(a, b, preferred_element_type=F32)


def mask_kernel(mask_ref, after, columns_ref):
    for l in range(columns_ref.shape[0]):
        columns_ref[l] = mask_columns(mask_ref, l)


def inner_kernel(columns_ref, halo_ref, keep_ref, near_row, far_row, forcing, lift, inverse, far_ref, start_ref, matrix_ref, jumps):
    layers, width, dofs = near_row.shape
    odd = lax.axis_index("cross") & 1
    near_at, far_at = odd, 1 - odd
    is_odd = odd == 1
    outward = pl.ds(pl.multiple_of((1 - odd) * dofs, 128), dofs)
    inward = pl.ds(pl.multiple_of(odd * dofs, 128), dofs)
    weights = lift[...].reshape(4 * dofs, dofs)
    far_carry = near_carry = None
    for l in range(layers):
        columns = columns_ref[l]
        column = lambda face, even, other: jnp.where(
            is_odd, columns[:, 2 * face[1] + other : 2 * face[1] + other + 1], columns[:, 2 * face[0] + even : 2 * face[0] + even + 1]
        )
        near, far = near_row[l].astype(F32), far_row[l].astype(F32)
        far_at_rows = pl.ds(2 * l * width, width)
        near_at_rows = pl.ds((2 * l + 1) * width, width)
        step = near - far
        jumps[far_at_rows, outward] = masked_jump(column((1, 0), 1, 0), halo_ref[l].astype(F32), far)
        jumps[far_at_rows, inward] = (column((0, 1), 1, 0) * step).astype(BF16)
        jumps[near_at_rows, outward] = (column((1, 0), 0, 1) * -step).astype(BF16)
        jumps[near_at_rows, inward] = jnp.zeros((width, dofs), BF16)
        for at, cells, even in ((far_at_rows, far, 1), (near_at_rows, near, 0)):
            low, up = along_b(cells)
            jumps[at, pl.ds(2 * dofs, dofs)] = masked_jump(column((2, 2), even, 1 - even), low, cells)
            jumps[at, pl.ds(3 * dofs, dofs)] = masked_jump(column((3, 3), even, 1 - even), up, cells)
        lifted = dot(jumps[pl.ds(2 * l * width, 2 * width), :], weights)
        near_source = forcing[l, near_at].astype(F32) + lifted[width:]
        far_source = forcing[l, far_at].astype(F32) + lifted[:width]
        near_solved = dot(near_source.astype(BF16), inverse[l, near_at])
        far_solved = dot(far_source.astype(BF16), inverse[l, far_at])
        matrix_ref[l] = dot(lift[odd], inverse[l, near_at]).astype(BF16)
        far_carry = far_solved if l == 0 else keep_ref[l : l + 1, :] * far_carry + far_solved
        near_carry = near_solved if l == 0 else keep_ref[l : l + 1, :] * near_carry + near_solved
        far_ref[l] = far_carry
        start_ref[l] = near_carry


def outer_kernel(halo_ref, columns_ref, near_row, start_ref, matrix_ref, keep_ref, far_ref, near_ref, p0, p3, p2, p1, carry):
    layers, width, dofs = near_row.shape
    cross = lax.axis_index("cross")
    odd = cross & 1
    inside = (cross != 0) & (cross != lax.axis_size("cross") - 1)
    total = None
    for l in range(layers):
        edge = jnp.where(odd == 1, columns_ref[l, :, 3:4], columns_ref[l, :, 0:1])
        halo = jnp.where(inside, halo_ref[l].astype(F32), 0.0)
        solved = dot(masked_jump(edge, halo, near_row[l].astype(F32)), matrix_ref[l])
        total = solved if l == 0 else keep_ref[l : l + 1, :] * total + solved
        near_ref[l] = start_ref[l] + total
    total = total + start_ref[layers - 1]
    carry[pl.ds(0, width), :] = far_ref[layers - 1]
    carry[pl.ds(width, width), :] = total
    factor = keep_ref[0:1, :]
    for l in range(1, layers):
        factor = factor * keep_ref[l : l + 1, :]
    high = factor.astype(BF16).astype(F32)
    low = factor - high
    at = lax.broadcasted_iota(jnp.int32, (8, dofs), 0)
    extra = jnp.where(at == 0, high, jnp.where(at == 1, low, 0.0))
    piece = 2 * width // GROUP
    member = lax.axis_index("stream") & (GROUP - 1)
    for k, out in enumerate((p0, p1, p2, p3)):
        start = pl.multiple_of((member ^ k) * piece, 8)
        out[...] = jnp.concatenate([carry[pl.ds(start, piece), :], extra], axis=0).astype(BF16)


def final_kernel(step, far_ref, near_ref, keep_ref, one, other, *rest):
    out_hbm, out, sem = rest[-3:]
    layers, width, dofs = far_ref.shape
    piece = one.shape[0]
    odd = lax.axis_index("cross") & 1
    member = lax.axis_index("stream") & (GROUP - 1)
    low = member < 2
    at = jnp.where(low, member, 3 - member) if step == 0 else jnp.where(low, 1 - member, member - 2)
    entering = [part[...].astype(F32) for part in (one, other)]
    entering = (jnp.where(low, entering[0], entering[1]), jnp.where(low, entering[1], entering[0]))
    starts = (pl.multiple_of(at * piece, 8), pl.multiple_of((1 - at) * piece, 8))
    copies = []
    factor = None
    for l in range(layers):
        factor = keep_ref[l : l + 1, :] if l == 0 else factor * keep_ref[l : l + 1, :]
        for i, (part, row) in enumerate(((far_ref, 1 - odd), (near_ref, odd))):
            span = pl.ds(starts[i], piece)
            out[l, i] = part[l, span, :] + factor * entering[i]
            copies.append(pltpu.make_async_copy(out.at[l, i], out_hbm.at[l, row, span, :], sem.at[l, i]))
            copies[-1].start()
    for copy in copies:
        copy.wait()


def call(kernel, operands, in_specs, outs, out_specs, scratch, flops, moved, aliases={}):
    return pl.pallas_call(
        kernel,
        out_shape=outs,
        in_specs=in_specs,
        out_specs=out_specs,
        scratch_shapes=scratch,
        input_output_aliases=aliases,
        compiler_params=pltpu.CompilerParams(vmem_limit_bytes=VMEM_LIMIT),
        cost_estimate=pl.CostEstimate(flops=flops, bytes_accessed=moved, transcendentals=0),
    )(*operands)


def body(forcing, cells, face_mask, lifting, inverse, retention):
    layers, _, width, dofs = cells.shape
    crosses, streams = lax.axis_size("cross"), lax.axis_size("stream")
    cross, stream = lax.axis_index("cross"), lax.axis_index("stream")
    odd, member = cross % 2, stream % GROUP

    links = []
    for s in range(streams):
        for c in range(crosses):
            other = (s ^ 1, c) if c in (0, crosses - 1) else (s, c + 1 if c % 2 else c - 1)
            links.append((s * crosses + c, other[0] * crosses + other[1]))
    vmem, hbm = pl.BlockSpec(memory_space=pltpu.VMEM), pl.BlockSpec(memory_space=pl.ANY)
    like = jax.ShapeDtypeStruct
    stack = like((layers, width, dofs), F32)
    slab = like((layers, width, dofs), BF16)
    unit = 2 * layers * width * dofs * dofs

    near_row = lax.dynamic_index_in_dim(cells, odd, 1, False)
    far_row = lax.dynamic_index_in_dim(lax.optimization_barrier((cells, near_row))[0], 1 - odd, 1, False)
    chip_halo = lax.ppermute(near_row, ("stream", "cross"), links)
    core_halo = lax.ppermute(far_row, "cross", [(i, i ^ 1) for i in range(crosses)])
    columns = call(
        mask_kernel, (face_mask, near_row), [vmem, hbm], like((layers, width, 128), F32), vmem, [], MASK_COST, 20_000_000
    )
    far, near_start, matrix = call(
        inner_kernel,
        (columns, core_halo, retention, near_row, far_row, forcing, lifting, inverse),
        [vmem] * 8,
        (stack, stack, like((layers, dofs, dofs), BF16)),
        (vmem,) * 3,
        [pltpu.VMEM((2 * layers * width, 4 * dofs), BF16)],
        9 * unit,
        5_000_000,
    )

    piece = 2 * width // GROUP
    near, piece0, piece3, piece2, piece1 = call(
        outer_kernel,
        (chip_halo, columns, near_row, near_start, matrix, retention, far),
        [vmem] * 7,
        (stack,) + (like((piece + 8, dofs), BF16),) * GROUP,
        (vmem,) * (1 + GROUP),
        [pltpu.VMEM((2 * width, dofs), F32)],
        2 * unit,
        3_000_000,
    )

    def swap(part, distance):
        return lax.ppermute(part, "stream", [(i, i ^ distance) for i in range(streams)])

    got = [piece0, swap(piece1, 1), swap(piece2, 2), swap(piece3, 3)]
    pick = lambda parts, j: functools.reduce(
        lambda rest, k: jnp.where((member ^ k) == j, parts[k], rest), range(1, GROUP), parts[0]
    )
    ordered = [pick(got, j).astype(F32) for j in range(GROUP)]
    values = [part[:piece] for part in ordered]
    factors = [part[piece : piece + 1] + part[piece + 1 : piece + 2] for part in ordered]

    total, total_factor = values[0], factors[0]
    for j in range(1, GROUP):
        total = factors[j] * total + values[j]
        total_factor = total_factor * factors[j]
    before, before_factor = jnp.zeros_like(total), jnp.ones_like(total_factor)
    distance = GROUP
    while distance < streams:
        later = (stream & distance) != 0
        if streams == 2 * GROUP:
            before = jnp.where(later, swap(total.astype(BF16), distance).astype(F32), before)
        else:
            met = swap(jnp.concatenate([total, total_factor], axis=0), distance)
            met, met_factor = met[:piece], met[piece:]
            before = jnp.where(later, before_factor * met + before, before)
            before_factor = jnp.where(later, before_factor * met_factor, before_factor)
            total = jnp.where(later, total_factor * met + total, met_factor * total + met)
            total_factor = total_factor * met_factor
        distance *= 2

    entering = [before]
    for j in range(GROUP - 1):
        entering.append(factors[j] * entering[j] + values[j])
    entering = [part.astype(BF16) for part in entering]
    give = [pick(entering, k) for k in range(GROUP)]
    back = [give[0]] + [swap(give[k], k) for k in range(1, GROUP)]

    result = like(cells.shape, F32)
    scratch = [pltpu.VMEM((layers, 2, piece, dofs), F32), pltpu.SemaphoreType.DMA((layers, 2))]
    half = call(
        functools.partial(final_kernel, 0), (far, near, retention, back[0], back[3]), [vmem] * 5, result, hbm, scratch, 500_000, 2_000_000
    )
    return call(
        functools.partial(final_kernel, 1),
        (far, near, retention, back[1], back[2], half),
        [vmem] * 5 + [hbm],
        result,
        hbm,
        scratch,
        500_000,
        2_000_000,
        {5: 0},
    )


def solution(mesh):
    return jax.shard_map(
        body,
        mesh=mesh,
        in_specs=(
            P("stream", "cross", None, None),
            P("stream", "cross", None, None),
            P(None, "stream", "cross", None),
            P(),
            P("stream", "cross", None, None),
            P("stream", None),
        ),
        out_specs=P("stream", "cross", None, None),
        check_vma=False,
    )
```

```python
import functools

import jax
import jax.numpy as jnp
from jax import lax
from jax.experimental import pallas as pl
from jax.experimental.pallas import tpu as pltpu
from jax.sharding import PartitionSpec as P

GROUP = 4
F32, BF16 = jnp.float32, jnp.bfloat16
VMEM_LIMIT = 24 * 1024 * 1024
MASK_COST = 10_000_000_000


def masked_jump(mask, neighbour, center):
    return (mask * (neighbour - center)).astype(BF16)


def along_b(cells):
    rows = lax.broadcasted_iota(jnp.int32, cells.shape, 0)
    last = cells.shape[0] - 1
    lower = jnp.where(rows == 0, 0.0, pltpu.roll(cells, 1, 0))
    upper = jnp.where(rows == last, 0.0, pltpu.roll(cells, last, 0))
    return lower, upper


def mask_columns(mask_ref, layer):
    rows = [mask_ref[face, layer, a : a + 1, :] for face in range(4) for a in range(2)]
    rows.append(jnp.zeros((120, rows[0].shape[1]), rows[0].dtype))
    return jnp.concatenate(rows, axis=0).astype(F32).T


def dot(a, b):
    return jnp.dot(a, b, preferred_element_type=F32)


def mask_kernel(mask_ref, after, columns_ref):
    for l in range(columns_ref.shape[0]):
        columns_ref[l] = mask_columns(mask_ref, l)


def inner_kernel(columns_ref, halo_ref, keep_ref, near_row, far_row, forcing, lift, inverse, far_ref, start_ref, matrix_ref, jumps):
    layers, width, dofs = near_row.shape
    odd = lax.axis_index("cross") & 1
    near_at, far_at = odd, 1 - odd
    is_odd = odd == 1
    outward = pl.ds(pl.multiple_of((1 - odd) * dofs, 128), dofs)
    inward = pl.ds(pl.multiple_of(odd * dofs, 128), dofs)
    weights = lift[...].reshape(4 * dofs, dofs)
    far_carry = near_carry = None
    for l in range(layers):
        columns = columns_ref[l]
        column = lambda face, even, other: jnp.where(
            is_odd, columns[:, 2 * face[1] + other : 2 * face[1] + other + 1], columns[:, 2 * face[0] + even : 2 * face[0] + even + 1]
        )
        near, far = near_row[l].astype(F32), far_row[l].astype(F32)
        far_at_rows = pl.ds(2 * l * width, width)
        near_at_rows = pl.ds((2 * l + 1) * width, width)
        step = near - far
        jumps[far_at_rows, outward] = masked_jump(column((1, 0), 1, 0), halo_ref[l].astype(F32), far)
        jumps[far_at_rows, inward] = (column((0, 1), 1, 0) * step).astype(BF16)
        jumps[near_at_rows, outward] = (column((1, 0), 0, 1) * -step).astype(BF16)
        jumps[near_at_rows, inward] = jnp.zeros((width, dofs), BF16)
        for at, cells, even in ((far_at_rows, far, 1), (near_at_rows, near, 0)):
            low, up = along_b(cells)
            jumps[at, pl.ds(2 * dofs, dofs)] = masked_jump(column((2, 2), even, 1 - even), low, cells)
            jumps[at, pl.ds(3 * dofs, dofs)] = masked_jump(column((3, 3), even, 1 - even), up, cells)
        lifted = dot(jumps[pl.ds(2 * l * width, 2 * width), :], weights)
        near_source = forcing[l, near_at].astype(F32) + lifted[width:]
        far_source = forcing[l, far_at].astype(F32) + lifted[:width]
        near_solved = dot(near_source.astype(BF16), inverse[l, near_at])
        far_solved = dot(far_source.astype(BF16), inverse[l, far_at])
        matrix_ref[l] = dot(lift[odd], inverse[l, near_at]).astype(BF16)
        far_carry = far_solved if l == 0 else keep_ref[l : l + 1, :] * far_carry + far_solved
        near_carry = near_solved if l == 0 else keep_ref[l : l + 1, :] * near_carry + near_solved
        far_ref[l] = far_carry
        start_ref[l] = near_carry


def outer_kernel(halo_ref, columns_ref, near_row, start_ref, matrix_ref, keep_ref, far_ref, near_ref, p0, p3, p2, p1, carry):
    layers, width, dofs = near_row.shape
    cross = lax.axis_index("cross")
    odd = cross & 1
    inside = (cross != 0) & (cross != lax.axis_size("cross") - 1)
    total = None
    for l in range(layers):
        edge = jnp.where(odd == 1, columns_ref[l, :, 3:4], columns_ref[l, :, 0:1])
        halo = jnp.where(inside, halo_ref[l].astype(F32), 0.0)
        solved = dot(masked_jump(edge, halo, near_row[l].astype(F32)), matrix_ref[l])
        total = solved if l == 0 else keep_ref[l : l + 1, :] * total + solved
        near_ref[l] = start_ref[l] + total
    total = total + start_ref[layers - 1]
    carry[pl.ds(0, width), :] = far_ref[layers - 1]
    carry[pl.ds(width, width), :] = total
    factor = keep_ref[0:1, :]
    for l in range(1, layers):
        factor = factor * keep_ref[l : l + 1, :]
    high = factor.astype(BF16).astype(F32)
    low = factor - high
    at = lax.broadcasted_iota(jnp.int32, (8, dofs), 0)
    extra = jnp.where(at == 0, high, jnp.where(at == 1, low, 0.0))
    piece = 2 * width // GROUP
    member = lax.axis_index("stream") & (GROUP - 1)
    for k, out in enumerate((p0, p1, p2, p3)):
        start = pl.multiple_of((member ^ k) * piece, 8)
        out[...] = jnp.concatenate([carry[pl.ds(start, piece), :], extra], axis=0).astype(BF16)


def final_kernel(step, far_ref, near_ref, keep_ref, one, other, *rest):
    out_hbm, out, sem = rest[-3:]
    layers, width, dofs = far_ref.shape
    piece = one.shape[0]
    odd = lax.axis_index("cross") & 1
    member = lax.axis_index("stream") & (GROUP - 1)
    low = member < 2
    at = jnp.where(low, member, 3 - member) if step == 0 else jnp.where(low, 1 - member, member - 2)
    entering = [part[...].astype(F32) for part in (one, other)]
    entering = (jnp.where(low, entering[0], entering[1]), jnp.where(low, entering[1], entering[0]))
    starts = (pl.multiple_of(at * piece, 8), pl.multiple_of((1 - at) * piece, 8))
    copies = []
    factor = None
    for l in range(layers):
        factor = keep_ref[l : l + 1, :] if l == 0 else factor * keep_ref[l : l + 1, :]
        for i, (part, row) in enumerate(((far_ref, 1 - odd), (near_ref, odd))):
            span = pl.ds(starts[i], piece)
            out[l, i] = part[l, span, :] + factor * entering[i]
            copies.append(pltpu.make_async_copy(out.at[l, i], out_hbm.at[l, row, span, :], sem.at[l, i]))
            copies[-1].start()
    for copy in copies:
        copy.wait()


def call(kernel, operands, in_specs, outs, out_specs, scratch, flops, moved, aliases={}):
    return pl.pallas_call(
        kernel,
        out_shape=outs,
        in_specs=in_specs,
        out_specs=out_specs,
        scratch_shapes=scratch,
        input_output_aliases=aliases,
        compiler_params=pltpu.CompilerParams(vmem_limit_bytes=VMEM_LIMIT),
        cost_estimate=pl.CostEstimate(flops=flops, bytes_accessed=moved, transcendentals=0),
    )(*operands)


def body(forcing, cells, face_mask, lifting, inverse, retention):
    layers, _, width, dofs = cells.shape
    crosses, streams = lax.axis_size("cross"), lax.axis_size("stream")
    cross, stream = lax.axis_index("cross"), lax.axis_index("stream")
    odd, member = cross % 2, stream % GROUP

    links = []
    for s in range(streams):
        for c in range(crosses):
            other = (s ^ 1, c) if c in (0, crosses - 1) else (s, c + 1 if c % 2 else c - 1)
            links.append((s * crosses + c, other[0] * crosses + other[1]))
    vmem, hbm = pl.BlockSpec(memory_space=pltpu.VMEM), pl.BlockSpec(memory_space=pl.ANY)
    like = jax.ShapeDtypeStruct
    stack = like((layers, width, dofs), F32)
    slab = like((layers, width, dofs), BF16)
    unit = 2 * layers * width * dofs * dofs

    near_row = lax.dynamic_index_in_dim(cells, odd, 1, False)
    far_row = lax.dynamic_index_in_dim(lax.optimization_barrier((cells, near_row))[0], 1 - odd, 1, False)
    chip_halo = lax.ppermute(near_row, ("stream", "cross"), links)
    core_halo = lax.ppermute(far_row, "cross", [(i, i ^ 1) for i in range(crosses)])
    columns = call(
        mask_kernel, (face_mask, near_row), [vmem, hbm], like((layers, width, 128), F32), vmem, [], MASK_COST, 20_000_000
    )
    far, near_start, matrix = call(
        inner_kernel,
        (columns, core_halo, retention, near_row, far_row, forcing, lifting, inverse),
        [vmem] * 8,
        (stack, stack, like((layers, dofs, dofs), BF16)),
        (vmem,) * 3,
        [pltpu.VMEM((2 * layers * width, 4 * dofs), BF16)],
        9 * unit,
        5_000_000,
    )

    piece = 2 * width // GROUP
    near, piece0, piece3, piece2, piece1 = call(
        outer_kernel,
        (chip_halo, columns, near_row, near_start, matrix, retention, far),
        [vmem] * 7,
        (stack,) + (like((piece + 8, dofs), BF16),) * GROUP,
        (vmem,) * (1 + GROUP),
        [pltpu.VMEM((2 * width, dofs), F32)],
        2 * unit,
        3_000_000,
    )

    def swap(part, distance):
        return lax.ppermute(part, "stream", [(i, i ^ distance) for i in range(streams)])

    got = [piece0, swap(piece1, 1), swap(piece2, 2), swap(piece3, 3)]
    even, low = member % 2 == 0, member < 2
    order = lambda mine, partner: (jnp.where(even, mine, partner), jnp.where(even, partner, mine))

    def unpack(part):
        part = part.astype(F32)
        return part[:piece], part[piece : piece + 1] + part[piece + 1 : piece + 2]

    def join(first, second):
        return second[1] * first[0] + second[0], first[1] * second[1]

    theirs = [unpack(part) for part in order(got[2], got[3])]
    *theirs_joined, partner = lax.optimization_barrier((*join(*theirs), got[1]))
    ours = [unpack(part) for part in order(got[0], partner)]
    ours_joined = join(*ours)
    total = jnp.where(low, theirs_joined[1] * ours_joined[0] + theirs_joined[0], ours_joined[1] * theirs_joined[0] + ours_joined[0])
    total_factor = ours_joined[1] * theirs_joined[1]

    def enter(pair, ahead, goes_first):
        own, share = jnp.where(goes_first, 0.0, ahead[0]), jnp.where(goes_first, 1.0, ahead[1])
        value, factor = pair[0]
        return zip(order(own, factor * own + value), order(share, factor * share))

    entries = [*enter(theirs, ours_joined, ~low), *enter(ours, theirs_joined, low)]
    entries = lax.optimization_barrier(entries)

    before, before_factor = jnp.zeros_like(total), jnp.ones_like(total_factor)
    distance = GROUP
    while distance < streams:
        later = (stream & distance) != 0
        if streams == 2 * GROUP:
            before = jnp.where(later, swap(total.astype(BF16), distance).astype(F32), before)
        else:
            met = swap(jnp.concatenate([total, total_factor], axis=0), distance)
            met, met_factor = met[:piece], met[piece:]
            before = jnp.where(later, before_factor * met + before, before)
            before_factor = jnp.where(later, before_factor * met_factor, before_factor)
            total = jnp.where(later, total_factor * met + total, met_factor * total + met)
            total_factor = total_factor * met_factor
        distance *= 2

    give = [(own + share * before).astype(BF16) for own, share in entries[2:] + entries[:2]]
    back = [give[0]] + [swap(give[k], k) for k in range(1, GROUP)]

    result = like(cells.shape, F32)
    scratch = [pltpu.VMEM((layers, 2, piece, dofs), F32), pltpu.SemaphoreType.DMA((layers, 2))]
    half = call(
        functools.partial(final_kernel, 0), (far, near, retention, back[0], back[3]), [vmem] * 5, result, hbm, scratch, 500_000, 2_000_000
    )
    return call(
        functools.partial(final_kernel, 1),
        (far, near, retention, back[1], back[2], half),
        [vmem] * 5 + [hbm],
        result,
        hbm,
        scratch,
        500_000,
        2_000_000,
        {5: 0},
    )


def solution(mesh):
    return jax.shard_map(
        body,
        mesh=mesh,
        in_specs=(
            P("stream", "cross", None, None),
            P("stream", "cross", None, None),
            P(None, "stream", "cross", None),
            P(),
            P("stream", "cross", None, None),
            P("stream", None),
        ),
        out_specs=P("stream", "cross", None, None),
        check_vma=False,
    )
```

```python
import functools

import jax
import jax.numpy as jnp
from jax import lax
from jax.experimental import pallas as pl
from jax.experimental.pallas import tpu as pltpu
from jax.sharding import PartitionSpec as P

GROUP = 4
F32, BF16 = jnp.float32, jnp.bfloat16
VMEM_LIMIT = 24 * 1024 * 1024
MASK_COST = 10_000_000_000


def masked_jump(mask, neighbour, center):
    return (mask * (neighbour - center)).astype(BF16)


def along_b(cells):
    rows = lax.broadcasted_iota(jnp.int32, cells.shape, 0)
    last = cells.shape[0] - 1
    lower = jnp.where(rows == 0, 0.0, pltpu.roll(cells, 1, 0))
    upper = jnp.where(rows == last, 0.0, pltpu.roll(cells, last, 0))
    return lower, upper


def mask_columns(mask_ref, layer):
    rows = [mask_ref[face, layer, a : a + 1, :] for face in range(4) for a in range(2)]
    rows.append(jnp.zeros((120, rows[0].shape[1]), rows[0].dtype))
    return jnp.concatenate(rows, axis=0).astype(F32).T


def dot(a, b):
    return jnp.dot(a, b, preferred_element_type=F32)


def mask_kernel(mask_ref, after, columns_ref):
    for l in range(columns_ref.shape[0]):
        columns_ref[l] = mask_columns(mask_ref, l)


def inner_kernel(columns_ref, halo_ref, keep_ref, near_row, far_row, forcing, lift, inverse, far_ref, start_ref, matrix_ref, jumps):
    layers, width, dofs = near_row.shape
    odd = lax.axis_index("cross") & 1
    near_at, far_at = odd, 1 - odd
    is_odd = odd == 1
    outward = pl.ds(pl.multiple_of((1 - odd) * dofs, 128), dofs)
    inward = pl.ds(pl.multiple_of(odd * dofs, 128), dofs)
    weights = lift[...].reshape(4 * dofs, dofs)
    far_carry = near_carry = None
    for l in range(layers):
        columns = columns_ref[l]
        column = lambda face, even, other: jnp.where(
            is_odd, columns[:, 2 * face[1] + other : 2 * face[1] + other + 1], columns[:, 2 * face[0] + even : 2 * face[0] + even + 1]
        )
        near, far = near_row[l].astype(F32), far_row[l].astype(F32)
        far_at_rows = pl.ds(2 * l * width, width)
        near_at_rows = pl.ds((2 * l + 1) * width, width)
        step = near - far
        jumps[far_at_rows, outward] = masked_jump(column((1, 0), 1, 0), halo_ref[l].astype(F32), far)
        jumps[far_at_rows, inward] = (column((0, 1), 1, 0) * step).astype(BF16)
        jumps[near_at_rows, outward] = (column((1, 0), 0, 1) * -step).astype(BF16)
        jumps[near_at_rows, inward] = jnp.zeros((width, dofs), BF16)
        for at, cells, even in ((far_at_rows, far, 1), (near_at_rows, near, 0)):
            low, up = along_b(cells)
            jumps[at, pl.ds(2 * dofs, dofs)] = masked_jump(column((2, 2), even, 1 - even), low, cells)
            jumps[at, pl.ds(3 * dofs, dofs)] = masked_jump(column((3, 3), even, 1 - even), up, cells)
        lifted = dot(jumps[pl.ds(2 * l * width, 2 * width), :], weights)
        near_source = forcing[l, near_at].astype(F32) + lifted[width:]
        far_source = forcing[l, far_at].astype(F32) + lifted[:width]
        near_solved = dot(near_source.astype(BF16), inverse[l, near_at])
        far_solved = dot(far_source.astype(BF16), inverse[l, far_at])
        matrix_ref[l] = dot(lift[odd], inverse[l, near_at]).astype(BF16)
        far_carry = far_solved if l == 0 else keep_ref[l : l + 1, :] * far_carry + far_solved
        near_carry = near_solved if l == 0 else keep_ref[l : l + 1, :] * near_carry + near_solved
        far_ref[l] = far_carry
        start_ref[l] = near_carry


def outer_kernel(halo_ref, columns_ref, near_row, start_ref, matrix_ref, keep_ref, far_ref, near_ref, p0, p3, p2, p1, carry):
    layers, width, dofs = near_row.shape
    cross = lax.axis_index("cross")
    odd = cross & 1
    inside = (cross != 0) & (cross != lax.axis_size("cross") - 1)
    total = None
    scale = jnp.where(inside, 1.0, 0.0).astype(BF16)
    for l in range(layers):
        edge = jnp.where(odd == 1, columns_ref[l, :, 3:4], columns_ref[l, :, 0:1])
        edge = jnp.broadcast_to(edge, (width, dofs)).astype(BF16)
        solved = dot(edge * (halo_ref[l] * scale - near_row[l]), matrix_ref[l])
        total = solved if l == 0 else keep_ref[l : l + 1, :] * total + solved
        near_ref[l] = start_ref[l] + total
    total = total + start_ref[layers - 1]
    carry[pl.ds(0, width), :] = far_ref[layers - 1]
    carry[pl.ds(width, width), :] = total
    factor = keep_ref[0:1, :]
    for l in range(1, layers):
        factor = factor * keep_ref[l : l + 1, :]
    high = factor.astype(BF16).astype(F32)
    low = factor - high
    at = lax.broadcasted_iota(jnp.int32, (8, dofs), 0)
    extra = jnp.where(at == 0, high, jnp.where(at == 1, low, 0.0))
    piece = 2 * width // GROUP
    member = lax.axis_index("stream") & (GROUP - 1)
    for k, out in enumerate((p0, p1, p2, p3)):
        start = pl.multiple_of((member ^ k) * piece, 8)
        out[...] = jnp.concatenate([carry[pl.ds(start, piece), :], extra], axis=0).astype(BF16)


def final_kernel(step, far_ref, near_ref, keep_ref, one, other, *rest):
    out_hbm, out, sem = rest[-3:]
    layers, width, dofs = far_ref.shape
    piece = one.shape[0]
    odd = lax.axis_index("cross") & 1
    member = lax.axis_index("stream") & (GROUP - 1)
    low = member < 2
    at = jnp.where(low, member, 3 - member) if step == 0 else jnp.where(low, 1 - member, member - 2)
    entering = [part[...].astype(F32) for part in (one, other)]
    entering = (jnp.where(low, entering[0], entering[1]), jnp.where(low, entering[1], entering[0]))
    starts = (pl.multiple_of(at * piece, 8), pl.multiple_of((1 - at) * piece, 8))
    copies = []
    factor = None
    for l in range(layers):
        factor = keep_ref[l : l + 1, :] if l == 0 else factor * keep_ref[l : l + 1, :]
        for i, (part, row) in enumerate(((far_ref, 1 - odd), (near_ref, odd))):
            span = pl.ds(starts[i], piece)
            out[l, i] = part[l, span, :] + factor * entering[i]
            copies.append(pltpu.make_async_copy(out.at[l, i], out_hbm.at[l, row, span, :], sem.at[l, i]))
            copies[-1].start()
    for copy in copies:
        copy.wait()


def call(kernel, operands, in_specs, outs, out_specs, scratch, flops, moved, aliases={}):
    return pl.pallas_call(
        kernel,
        out_shape=outs,
        in_specs=in_specs,
        out_specs=out_specs,
        scratch_shapes=scratch,
        input_output_aliases=aliases,
        compiler_params=pltpu.CompilerParams(vmem_limit_bytes=VMEM_LIMIT),
        cost_estimate=pl.CostEstimate(flops=flops, bytes_accessed=moved, transcendentals=0),
    )(*operands)


def body(forcing, cells, face_mask, lifting, inverse, retention):
    layers, _, width, dofs = cells.shape
    crosses, streams = lax.axis_size("cross"), lax.axis_size("stream")
    cross, stream = lax.axis_index("cross"), lax.axis_index("stream")
    odd, member = cross % 2, stream % GROUP

    links = []
    for s in range(streams):
        for c in range(crosses):
            other = (s ^ 1, c) if c in (0, crosses - 1) else (s, c + 1 if c % 2 else c - 1)
            links.append((s * crosses + c, other[0] * crosses + other[1]))
    vmem, hbm = pl.BlockSpec(memory_space=pltpu.VMEM), pl.BlockSpec(memory_space=pl.ANY)
    like = jax.ShapeDtypeStruct
    stack = like((layers, width, dofs), F32)
    slab = like((layers, width, dofs), BF16)
    unit = 2 * layers * width * dofs * dofs

    near_row = lax.dynamic_index_in_dim(cells, odd, 1, False)
    far_row = lax.dynamic_index_in_dim(lax.optimization_barrier((cells, near_row))[0], 1 - odd, 1, False)
    chip_halo = lax.ppermute(near_row, ("stream", "cross"), links)
    core_halo = lax.ppermute(far_row, "cross", [(i, i ^ 1) for i in range(crosses)])
    columns = call(
        mask_kernel, (face_mask, near_row), [vmem, hbm], like((layers, width, 128), F32), vmem, [], MASK_COST, 20_000_000
    )
    far, near_start, matrix = call(
        inner_kernel,
        (columns, core_halo, retention, near_row, far_row, forcing, lifting, inverse),
        [vmem] * 8,
        (stack, stack, like((layers, dofs, dofs), BF16)),
        (vmem,) * 3,
        [pltpu.VMEM((2 * layers * width, 4 * dofs), BF16)],
        9 * unit,
        5_000_000,
    )

    piece = 2 * width // GROUP
    near, piece0, piece3, piece2, piece1 = call(
        outer_kernel,
        (chip_halo, columns, near_row, near_start, matrix, retention, far),
        [vmem] * 7,
        (stack,) + (like((piece + 8, dofs), BF16),) * GROUP,
        (vmem,) * (1 + GROUP),
        [pltpu.VMEM((2 * width, dofs), F32)],
        2 * unit,
        3_000_000,
    )

    def swap(part, distance):
        return lax.ppermute(part, "stream", [(i, i ^ distance) for i in range(streams)])

    got = [piece0, swap(piece1, 1), swap(piece2, 2), swap(piece3, 3)]
    even, low = member % 2 == 0, member < 2
    order = lambda mine, partner: (jnp.where(even, mine, partner), jnp.where(even, partner, mine))

    def unpack(part):
        part = part.astype(F32)
        return part[:piece], part[piece : piece + 1] + part[piece + 1 : piece + 2]

    def join(first, second):
        return second[1] * first[0] + second[0], first[1] * second[1]

    theirs = [unpack(part) for part in order(got[2], got[3])]
    *theirs_joined, partner = lax.optimization_barrier((*join(*theirs), got[1]))
    ours = [unpack(part) for part in order(got[0], partner)]
    ours_joined = join(*ours)
    total = jnp.where(low, theirs_joined[1] * ours_joined[0] + theirs_joined[0], ours_joined[1] * theirs_joined[0] + ours_joined[0])
    total_factor = ours_joined[1] * theirs_joined[1]

    def enter(pair, ahead, goes_first):
        own, share = jnp.where(goes_first, 0.0, ahead[0]), jnp.where(goes_first, 1.0, ahead[1])
        value, factor = pair[0]
        return zip(order(own, factor * own + value), order(share, factor * share))

    entries = [*enter(theirs, ours_joined, ~low), *enter(ours, theirs_joined, low)]
    entries = lax.optimization_barrier(entries)

    before, before_factor = jnp.zeros_like(total), jnp.ones_like(total_factor)
    distance = GROUP
    while distance < streams:
        later = (stream & distance) != 0
        if streams == 2 * GROUP:
            before = jnp.where(later, swap(total.astype(BF16), distance).astype(F32), before)
        else:
            met = swap(jnp.concatenate([total, total_factor], axis=0), distance)
            met, met_factor = met[:piece], met[piece:]
            before = jnp.where(later, before_factor * met + before, before)
            before_factor = jnp.where(later, before_factor * met_factor, before_factor)
            total = jnp.where(later, total_factor * met + total, met_factor * total + met)
            total_factor = total_factor * met_factor
        distance *= 2

    give = [(own + share * before).astype(BF16) for own, share in entries[2:] + entries[:2]]
    back = [give[0]] + [swap(give[k], k) for k in range(1, GROUP)]

    result = like(cells.shape, F32)
    scratch = [pltpu.VMEM((layers, 2, piece, dofs), F32), pltpu.SemaphoreType.DMA((layers, 2))]
    half = call(
        functools.partial(final_kernel, 0), (far, near, retention, back[0], back[3]), [vmem] * 5, result, hbm, scratch, 500_000, 2_000_000
    )
    return call(
        functools.partial(final_kernel, 1),
        (far, near, retention, back[1], back[2], half),
        [vmem] * 5 + [hbm],
        result,
        hbm,
        scratch,
        500_000,
        2_000_000,
        {5: 0},
    )


def solution(mesh):
    return jax.shard_map(
        body,
        mesh=mesh,
        in_specs=(
            P("stream", "cross", None, None),
            P("stream", "cross", None, None),
            P(None, "stream", "cross", None),
            P(),
            P("stream", "cross", None, None),
            P("stream", None),
        ),
        out_specs=P("stream", "cross", None, None),
        check_vma=False,
    )
```
